256 devices in a mesh: dp: 32 (over x, y, core), tensor: 8 (over z).
Axes of the slice: x: 4, y: 4, z: 8, core: 2. Of those that a mesh axis runs over, the one named last changes fastest.
Arguments:
- grad_key: float32 [32, 4096, 1024], P('dp', None, 'tensor'), as said below
- grad_value: float32 [32, 4096, 1024], P('dp', None, 'tensor'), as said below
- error_key: float32 [32, 4096, 1024], P('dp', None, 'tensor'), may hold values from -3 to 3
- error_value: float32 [32, 4096, 1024], P('dp', None, 'tensor'), may hold values from -3 to 3
- factor_key: float32 [1024, 32], P('tensor'), may hold values from -6 to 6
- factor_value: float32 [1024, 32], P('tensor'), may hold values from -6 to 6
Outputs:
- factor_key_new: float32 [1024, 32], P('tensor')
- factor_value_new: float32 [1024, 32], P('tensor')
- error_key_new: float32 [32, 4096, 1024], P('dp', None, 'tensor')
- error_value_new: float32 [32, 4096, 1024], P('dp', None, 'tensor')
The draws below stay inside these ranges and needn't reach their ends.
Inputs may be any that keep to these rules, and one draw needn't show every extreme that they name: `grad_key`: float32 gradients of order one to some tens. `grad_value`: float32 gradients of order one to some tens.
All inputs are finite; a program needn't handle non-finite values.
Results may differ from the reference program's by a relative error of at most 0.0001.
Values sent between devices are 32-bit elements; how exact they have to be, the bound alone decides.
A program may use at most 64 MiB of HBM per device.

```python
import jax
import jax.numpy as jnp
from jax import lax

D = 4096
KVD = 1024
RANK = 32
REPLICAS = 32


def gradient_like(key, noise, top):
    row_key, col_key = jax.random.split(key)
    rows = jnp.exp(jax.random.uniform(row_key, (1, D, 1), jnp.float32) * jnp.log(top))
    columns = jnp.exp(jax.random.uniform(col_key, (1, 1, KVD), jnp.float32) * jnp.log(top)) / jnp.sqrt(top)
    return noise * rows * columns


def draw_grad_key(key, part):
    key = jax.random.fold_in(key, 11)
    noise_key, scale_key = jax.random.split(key)
    noise = jnp.clip(jax.random.normal(noise_key, (REPLICAS, D, KVD), jnp.float32), -4.0, 4.0)
    return gradient_like(scale_key, noise, 10.0)


def draw_grad_value(key, part):
    key = jax.random.fold_in(key, 23)
    noise_key, scale_key = jax.random.split(key)
    noise = jnp.clip(jax.random.normal(noise_key, (REPLICAS, D, KVD), jnp.float32), -4.0, 4.0)
    return gradient_like(scale_key, noise, 10.0)


def steps_of(rng, shape, cuts, low, high):
    loudness, own = 1.0, jax.random.fold_in(rng, 6)
    for dim, shards_of in cuts:
        heights = jnp.exp(jax.random.uniform(jax.random.fold_in(own, dim), (shards_of,), jnp.float32, low / len(cuts), high / len(cuts)))
        loudness = loudness * jnp.repeat(heights, shape[dim] // shards_of).reshape([-1 if axis == dim else 1 for axis in range(len(shape))])
    return loudness


def scatter_about(rng, shape, scale, limit, cuts=(), held_as=jnp.bfloat16):
    entries = jax.random.normal(rng, shape, jnp.float32) * scale
    if len(cuts) > 0:
        entries = steps_of(rng, shape, cuts, -0.22, 0.18) * entries
    return jnp.clip(entries, min=-limit, max=limit).astype(held_as)


def setup_inputs(seed: int = 0) -> dict:
    key_of = jax.random.split(jax.random.key(seed), 7)
    return {
        "grad_key": draw_grad_key(jax.random.fold_in(key_of[6], 71), 0),
        "grad_value": draw_grad_value(jax.random.fold_in(key_of[6], 71), 0),
        "error_key": scatter_about(key_of[2], (REPLICAS, D, KVD), 0.5, 3.0, ((0, 32), (2, 8)), jnp.float32),
        "error_value": scatter_about(key_of[3], (REPLICAS, D, KVD), 0.5, 3.0, ((0, 32), (2, 8)), jnp.float32),
        "factor_key": scatter_about(key_of[4], (KVD, RANK), 1.0, 6.0, ((0, 8),), jnp.float32),
        "factor_value": scatter_about(key_of[5], (KVD, RANK), 1.0, 6.0, ((0, 8),), jnp.float32),
    }


def compress(gradient, residue, factor):
    highest = lax.Precision.HIGHEST

    def add_left(running, inputs):
        matrix = inputs[0] + inputs[1]
        return (running + jnp.dot(matrix, factor, precision=highest), None)
    left_factor, _ = lax.scan(add_left, jnp.zeros((D, RANK), jnp.float32), (gradient, residue))
    gram_matrix = jnp.dot(left_factor.T, left_factor, precision=highest)
    lower_factor = jnp.linalg.cholesky(gram_matrix)
    ortho_basis = lax.linalg.triangular_solve(lower_factor, left_factor, left_side=False, lower=True, transpose_a=True)

    def add_right(running, inputs):
        matrix = inputs[0] + inputs[1]
        return (running + jnp.dot(matrix.T, ortho_basis, precision=highest), None)
    right_factor, _ = lax.scan(add_right, jnp.zeros((KVD, RANK), jnp.float32), (gradient, residue))
    right_factor = right_factor / REPLICAS
    low_rank = jnp.dot(ortho_basis, right_factor.T, precision=highest)
    new_error = gradient + residue - low_rank[None]
    return (right_factor, new_error)

def reference(grad_key, grad_value, error_key, error_value, factor_key, factor_value):
    factor_key_new, error_key_new = compress(grad_key, error_key, factor_key)
    factor_value_new, error_value_new = compress(grad_value, error_value, factor_value)
    return (factor_key_new, factor_value_new, error_key_new, error_value_new)
```

```python
import functools

import jax
import jax.numpy as jnp
from jax import lax
from jax.experimental import pallas as pl
from jax.experimental.pallas import tpu as pltpu
from jax.sharding import PartitionSpec as P

MESH = pl.DeviceIdType.MESH
F32 = jnp.float32
BF16 = jnp.bfloat16
D = 4096
F = 128
RANK = 32
SUPERS = 8
ROWS = D // SUPERS
SUB = ROWS // 128
CHIPS = 32
PLANE = 16
QUADS = 4


def nt(a, b):
    return lax.dot_general(a, b, (((1,), (1,)), ((), ())), preferred_element_type=F32)


def nn(a, b):
    return jnp.dot(a, b, preferred_element_type=F32)


def full(a, b):
    return jnp.dot(a, b, preferred_element_type=F32, precision=lax.Precision.HIGHEST)


def split(value):
    high = value.astype(BF16)
    return high, (value - high.astype(F32)).astype(BF16)


def reduce_kernel(
    gk, gv, ek, ev, qk, qv,
    fed, left_rows, weight, right,
    stage, fed_high, fed_low, q_all, part, pair_in, ring_in, quad_in, left, acc_high, acc_low,
    t_part, t_pair, t_plane, t_sum,
    load_sem, pair_send, pair_recv, ring_send, ring_recv, quad_send, quad_recv,
    gather_send, gather_recv, pass_send, pass_recv, t_send, t_recv,
):
    dp = lax.axis_index("dp")
    z = lax.axis_index("tensor")
    core = dp % 2
    chip = dp // 2
    x = chip // 4
    y = chip % 4
    bit = z % 2
    quad = z // 2
    me = chip * 2 + bit
    base = me // SUB
    partner = (chip * 2 + 1 - core, z)

    def chip_of(member):
        return ((member // 2) * 2 + core, quad * 2 + member % 2)

    def member_at(offset):
        return (((x + offset // 8) % 4) * 4 + (y + (offset // 2) % 4) % 4) * 2 + (bit + offset % 2) % 2

    def block(step):
        return (base + 2 + step) % SUPERS

    def load(step, a, ref):
        rows = pl.ds(pl.multiple_of(block(step) * ROWS, ROWS), ROWS)
        return pltpu.make_async_copy(ref.at[0, rows], stage.at[a, rows], load_sem.at[step, a])

    def start_load(step, carry):
        for a, ref in enumerate((gk, gv, ek, ev)):
            load(step, a, ref).start()
        return carry

    lax.fori_loop(0, SUPERS, start_load, 0)

    barrier = pltpu.get_barrier_semaphore()

    def greet(i, carry):
        pl.semaphore_signal(barrier, inc=1, device_id=chip_of(member_at(i)), device_id_type=MESH)
        return carry

    lax.fori_loop(1, CHIPS, greet, 0)
    for i in range(1, QUADS):
        pl.semaphore_signal(barrier, inc=1, device_id=(dp, ((quad + i) % QUADS) * 2 + bit), device_id_type=MESH)
    pl.semaphore_signal(barrier, inc=1, device_id=partner, device_id_type=MESH)

    q_all[...] = jnp.zeros_like(q_all)
    for m, q in enumerate((qk, qv)):
        for part_of, piece in enumerate(split(q[...])):
            row = part_of * 2 * RANK + m * RANK
            q_all[row : row + RANK, m * F : (m + 1) * F] = piece

    def add_left(step, carry):
        b = block(step)
        rows = pl.ds(pl.multiple_of(b * ROWS, ROWS), ROWS)
        for a, ref in enumerate((gk, gv, ek, ev)):
            load(step, a, ref).wait()
        highs, lows = [], []
        for m in range(2):
            value = stage[m, rows, :] + stage[2 + m, rows, :]
            fed[rows, m * F : (m + 1) * F] = value
            high, low = split(value)
            fed_high[rows, m * F : (m + 1) * F] = high
            fed_low[rows, m * F : (m + 1) * F] = low
            highs.append(high)
            lows.append(low)
        high = jnp.concatenate(highs, axis=1)
        low = jnp.concatenate(lows, axis=1)
        product = nt(q_all[...], high)
        total = product[: 2 * RANK] + product[2 * RANK :] + nt(q_all[: 2 * RANK, :], low)
        for m in range(2):
            for j in range(SUB):
                part[m, b * SUB + j] = total[m * RANK : (m + 1) * RANK, j * 128 : (j + 1) * 128]
        return carry

    lax.fori_loop(0, SUPERS, add_left, 0)
    pl.semaphore_wait(barrier, CHIPS - 1 + QUADS - 1 + 1)

    def pair_copy(step):
        at = pl.ds(block(step) * SUB, SUB)
        return pltpu.make_async_remote_copy(
            src_ref=part.at[1 - core, at], dst_ref=pair_in.at[at], send_sem=pair_send.at[step],
            recv_sem=pair_recv.at[step], device_id=partner, device_id_type=MESH)

    def start_pair(step, carry):
        pair_copy(step).start()
        return carry

    lax.fori_loop(0, SUPERS, start_pair, 0)

    def ring_copy(member):
        return pltpu.make_async_remote_copy(
            src_ref=part.at[core, member], dst_ref=ring_in.at[me], send_sem=ring_send,
            recv_sem=ring_recv, device_id=chip_of(member), device_id_type=MESH)

    def scatter(step, carry):
        pair_copy(step).wait_recv()
        b = block(step)
        for j in range(SUB):
            member = b * SUB + j
            part[core, member] = part[core, member] + pair_in[member]

            @pl.when(member != me)
            def _():
                ring_copy(member).start()
        return carry

    lax.fori_loop(0, SUPERS, scatter, 0)
    ring_in[me] = part[core, me]
    most = pl.ds(0, CHIPS - 1)
    pltpu.make_async_copy(ring_in.at[most], ring_in.at[most], ring_recv).wait()
    quad_in[quad] = jnp.sum(ring_in[...], axis=0)

    def quad_copy(i):
        return pltpu.make_async_remote_copy(
            src_ref=quad_in.at[quad], dst_ref=quad_in.at[quad], send_sem=quad_send, recv_sem=quad_recv,
            device_id=(dp, ((quad + i) % QUADS) * 2 + bit), device_id_type=MESH)

    for i in (2, 1, 3):
        quad_copy(i).start()
    three = pl.ds(0, QUADS - 1)
    pltpu.make_async_copy(quad_in.at[three], quad_in.at[three], quad_recv).wait()
    left[core, me] = (quad_in[0] + quad_in[1]) + (quad_in[2] + quad_in[3])

    def gather_copy(member, slot):
        return pltpu.make_async_remote_copy(
            src_ref=left.at[core, slot], dst_ref=left.at[core, slot], send_sem=gather_send,
            recv_sem=gather_recv.at[slot], device_id=chip_of(member), device_id_type=MESH)

    def pass_copy(slot):
        return pltpu.make_async_remote_copy(
            src_ref=left.at[core, slot], dst_ref=left.at[core, slot], send_sem=pass_send,
            recv_sem=pass_recv.at[slot], device_id=partner, device_id_type=MESH)

    def start_gather(i, carry):
        offset = (i + CHIPS // 2) % CHIPS

        @pl.when(offset != 0)
        def _():
            gather_copy(member_at(offset), me).start()
        return carry

    lax.fori_loop(0, CHIPS, start_gather, 0)
    pass_copy(me).start()

    def near(step):
        turn = step // 2
        dx = turn + (turn // 2) * (1 - 2 * (turn % 2))
        return ((x + dx) % 4) * 2 + (base + step) % 2

    def forward(step):
        for j in range(SUB):
            slot = near(step) * SUB + j

            @pl.when(slot != me)
            def _():
                gather_copy(me, slot).wait_recv()
                pass_copy(slot).start()

    def left_block(b):
        sides = []
        for m in range(2):
            sides.append(jnp.concatenate([left[m, b * SUB + j] for j in range(SUB)], axis=1))
        return jnp.concatenate(sides, axis=0)

    def add_right(step):
        b = near(step)
        for j in range(SUB):
            slot = b * SUB + j
            pltpu.make_async_remote_copy(
                src_ref=left.at[1 - core, slot], dst_ref=left.at[1 - core, slot], send_sem=pass_send,
                recv_sem=pass_recv.at[slot], device_id=partner, device_id_type=MESH).wait_recv()
        rows = pl.ds(pl.multiple_of(b * ROWS, ROWS), ROWS)
        high, low = split(left_block(b))
        acc_high[...] += nn(jnp.concatenate([high, low], axis=0), fed_high[rows, :])
        acc_low[...] += nn(high, fed_low[rows, :])

    acc_high[...] = jnp.zeros_like(acc_high)
    acc_low[...] = jnp.zeros_like(acc_low)
    forward(0)

    def gather_step(step, carry):
        forward(step)
        add_right(step - 1)
        return carry

    lax.fori_loop(1, SUPERS, gather_step, 0)
    add_right(SUPERS - 1)
    for m in range(2):
        r, s = slice(m * RANK, (m + 1) * RANK), slice((m + 2) * RANK, (m + 3) * RANK)
        f = slice(m * F, (m + 1) * F)
        t_part[m] = acc_high[r, f] + acc_high[s, f] + acc_low[r, f]

    t_first = pltpu.make_async_remote_copy(
        src_ref=t_part.at[1 - core], dst_ref=t_pair, send_sem=t_send.at[0], recv_sem=t_recv.at[0],
        device_id=partner, device_id_type=MESH)
    t_first.start()

    def gram_step(b, total):
        high, low = split(left_block(b))
        both = jnp.concatenate([high, low], axis=0)
        return total + nt(both, both)

    t_first.wait_recv()
    t_plane[chip] = t_part[core] + t_pair[...]

    def plane_copy(i):
        other = ((x + i // 4) % 4) * 4 + (y + i % 4) % 4
        return pltpu.make_async_remote_copy(
            src_ref=t_plane.at[chip], dst_ref=t_plane.at[chip], send_sem=t_send.at[1], recv_sem=t_recv.at[1],
            device_id=(other * 2 + core, z), device_id_type=MESH)

    def start_plane(i, carry):
        offset = (i + PLANE // 2) % PLANE

        @pl.when(offset != 0)
        def _():
            plane_copy(offset).start()
        return carry

    lax.fori_loop(0, PLANE, start_plane, 0)

    products = lax.fori_loop(0, SUPERS, gram_step, jnp.zeros((4 * RANK, 4 * RANK), F32))
    top, bottom = products[: 2 * RANK], products[2 * RANK :]
    gram = top[:, : 2 * RANK] + top[:, 2 * RANK :] + bottom[:, : 2 * RANK] + bottom[:, 2 * RANK :]
    row = lax.broadcasted_iota(jnp.int32, (RANK, RANK), 0)
    column = lax.broadcasted_iota(jnp.int32, (RANK, RANK), 1)
    unit = jnp.where(row == column, 1.0, 0.0).astype(F32)
    work = jnp.concatenate([gram[:RANK, :RANK], unit, gram[RANK:, RANK:], unit], axis=1)
    wide_row = lax.broadcasted_iota(jnp.int32, (RANK, 4 * RANK), 0)
    wide_column = lax.broadcasted_iota(jnp.int32, (RANK, 4 * RANK), 1)
    first = wide_column < 2 * RANK
    pivots = jnp.ones((RANK, 4 * RANK), F32)
    for j in range(RANK):
        picked = jnp.where(first, work[:, j : j + 1], work[:, 2 * RANK + j : 2 * RANK + j + 1])
        pivot = picked[j : j + 1, :]
        pivots = jnp.where(wide_row == j, pivot, pivots)
        work = work - jnp.where(wide_row > j, picked / pivot, 0.0) * work[j : j + 1, :]
    inverse = work * lax.rsqrt(pivots)
    key_inverse = jnp.where((wide_column >= RANK) & first, inverse, 0.0)
    value_inverse = jnp.where(wide_column >= 3 * RANK, inverse, 0.0)
    lower = jnp.concatenate([key_inverse, value_inverse, jnp.zeros((2 * RANK, 4 * RANK), F32)], axis=0)
    upper = lower.T

    def turn_step(b, carry):
        for m in range(SUB):
            slot = b * SUB + m
            value = jnp.concatenate([left[0, slot], left[1, slot]], axis=0)
            high, low = split(value)
            both = jnp.concatenate([high.astype(F32), low.astype(F32)], axis=0)
            left_rows[pl.ds(pl.multiple_of(slot * 128, 128), 128), :] = both.T.astype(BF16)
        return carry

    lax.fori_loop(0, SUPERS, turn_step, 0)

    fifteen = pl.ds(0, PLANE - 1)
    pltpu.make_async_copy(t_plane.at[fifteen], t_plane.at[fifteen], t_recv.at[1]).wait()
    t_sum[core] = jnp.sum(t_plane[...], axis=0)
    t_last = pltpu.make_async_remote_copy(
        src_ref=t_sum.at[core], dst_ref=t_sum.at[core], send_sem=t_send.at[2], recv_sem=t_recv.at[2],
        device_id=partner, device_id_type=MESH)
    t_last.start()
    t_last.wait_recv()
    none = jnp.zeros((RANK, F), F32)
    sums = jnp.concatenate([none, t_sum[0], none, t_sum[1]], axis=0) * (1.0 / 32)
    right_rows = full(lower, sums)
    solved = full(upper, right_rows)
    right[...] = right_rows[: 2 * RANK]
    weight[: RANK, :] = solved[RANK : 2 * RANK]
    weight[RANK:, :] = solved[3 * RANK :]

    def end_pair(step, carry):
        pair_copy(step).wait_send()
        return carry

    lax.fori_loop(0, SUPERS, end_pair, 0)
    pltpu.make_async_copy(ring_in.at[most], ring_in.at[most], ring_send).wait()
    pltpu.make_async_copy(quad_in.at[three], quad_in.at[three], quad_send).wait()
    pltpu.make_async_copy(ring_in.at[most], ring_in.at[most], gather_send).wait()
    pltpu.make_async_copy(ring_in, ring_in, pass_send).wait()
    t_first.wait_send()
    pltpu.make_async_copy(t_plane.at[fifteen], t_plane.at[fifteen], t_send.at[1]).wait()
    t_last.wait_send()


def error_kernel(fed, left_rows, weight, right, right_key, right_value, new_key, new_value, wide, out, sem):
    right_key[...] = right[:RANK]
    right_value[...] = right[RANK:]
    wide[...] = jnp.zeros_like(wide)
    for part_of, piece in enumerate(split(weight[...])):
        for again in range(2):
            row = (2 * part_of + again) * 2 * RANK
            wide[row : row + RANK, :F] = piece[:RANK]
            wide[row + RANK : row + 2 * RANK, F:] = piece[RANK:]
    copies = []
    for b in range(SUPERS):
        rows = slice(b * ROWS, (b + 1) * ROWS)
        tall = left_rows[rows, :]
        change = nn(jnp.concatenate([tall, tall], axis=1), wide[...])
        for m, new in enumerate((new_key, new_value)):
            out[m, rows, :] = fed[rows, m * F : (m + 1) * F] - change[:, m * F : (m + 1) * F]
            copy = pltpu.make_async_copy(out.at[m, rows], new.at[0, rows], sem.at[b, m])
            copy.start()
            copies.append(copy)
    for copy in copies:
        copy.wait()


def on_device(grad_key, grad_value, error_key, error_value, factor_key, factor_value):
    vmem = pl.BlockSpec(memory_space=pltpu.VMEM)
    anywhere = pl.BlockSpec(memory_space=pl.ANY)
    dma = pltpu.SemaphoreType.DMA
    fed, left_rows, weight, right = pl.pallas_call(
        reduce_kernel,
        out_shape=(
            jax.ShapeDtypeStruct((D, 2 * F), F32),
            jax.ShapeDtypeStruct((D, 4 * RANK), BF16),
            jax.ShapeDtypeStruct((2 * RANK, F), F32),
            jax.ShapeDtypeStruct((2 * RANK, F), F32),
        ),
        in_specs=[pl.BlockSpec(memory_space=pltpu.HBM)] * 4 + [vmem] * 2,
        out_specs=(vmem,) * 4,
        scratch_shapes=[
            pltpu.VMEM((4, D, F), F32),
            pltpu.VMEM((D, 2 * F), BF16),
            pltpu.VMEM((D, 2 * F), BF16),
            pltpu.VMEM((4 * RANK, 2 * F), BF16),
            pltpu.VMEM((2, CHIPS, RANK, 128), F32),
            pltpu.VMEM((CHIPS, RANK, 128), F32),
            pltpu.VMEM((CHIPS, RANK, 128), F32),
            pltpu.VMEM((QUADS, RANK, 128), F32),
            pltpu.VMEM((2, CHIPS, RANK, 128), F32),
            pltpu.VMEM((4 * RANK, 2 * F), F32),
            pltpu.VMEM((2 * RANK, 2 * F), F32),
            pltpu.VMEM((2, RANK, F), F32),
            pltpu.VMEM((RANK, F), F32),
            pltpu.VMEM((PLANE, RANK, F), F32),
            pltpu.VMEM((2, RANK, F), F32),
            dma((SUPERS, 4)),
            dma((SUPERS,)),
            dma((SUPERS,)),
            dma,
            dma,
            dma,
            dma,
            dma,
            dma((CHIPS,)),
            dma,
            dma((CHIPS,)),
            dma((3,)),
            dma((3,)),
        ],
        compiler_params=pltpu.CompilerParams(
            collective_id=0, has_side_effects=True, vmem_limit_bytes=32 * 2**20
        ),
        cost_estimate=pl.CostEstimate(flops=10**9, bytes_accessed=12 * 2**20, transcendentals=0),
        name="reduce_factors",
    )(grad_key, grad_value, error_key, error_value, factor_key.T, factor_value.T)
    right_key, right_value, new_key, new_value = pl.pallas_call(
        error_kernel,
        out_shape=(
            jax.ShapeDtypeStruct((RANK, F), F32),
            jax.ShapeDtypeStruct((RANK, F), F32),
            jax.ShapeDtypeStruct((1, D, F), F32),
            jax.ShapeDtypeStruct((1, D, F), F32),
        ),
        in_specs=[vmem] * 4,
        out_specs=(vmem, vmem, anywhere, anywhere),
        scratch_shapes=[
            pltpu.VMEM((8 * RANK, 2 * F), BF16),
            pltpu.VMEM((2, D, F), F32),
            dma((SUPERS, 2)),
        ],
        compiler_params=pltpu.CompilerParams(vmem_limit_bytes=32 * 2**20),
        cost_estimate=pl.CostEstimate(flops=10**9, bytes_accessed=8 * 2**20, transcendentals=0),
        name="new_errors",
    )(fed, left_rows, weight, right)
    return right_key.T, right_value.T, new_key, new_value


def solution(mesh):
    in_specs = (
        P("dp", None, "tensor"),
        P("dp", None, "tensor"),
        P("dp", None, "tensor"),
        P("dp", None, "tensor"),
        P("tensor", None),
        P("tensor", None),
    )
    out_specs = (
        P("tensor", None),
        P("tensor", None),
        P("dp", None, "tensor"),
        P("dp", None, "tensor"),
    )
    return jax.shard_map(
        on_device, mesh=mesh, in_specs=in_specs, out_specs=out_specs, check_vma=False
    )
```

```python
import functools

import jax
import jax.numpy as jnp
from jax import lax
from jax.experimental import pallas as pl
from jax.experimental.pallas import tpu as pltpu
from jax.sharding import PartitionSpec as P

MESH = pl.DeviceIdType.MESH
F32 = jnp.float32
BF16 = jnp.bfloat16
D = 4096
F = 128
RANK = 32
SUPERS = 8
ROWS = D // SUPERS
SUB = ROWS // 128
CHIPS = 32
PLANE = 16
QUADS = 4
OFFSETS = sorted(
    [(dx, dy, dz) for dx in range(4) for dy in range(4) for dz in range(2) if dx + dy + dz > 0],
    key=lambda o: -(min(o[0], 4 - o[0]) + min(o[1], 4 - o[1]) + o[2]),
)


def nt(a, b):
    return lax.dot_general(a, b, (((1,), (1,)), ((), ())), preferred_element_type=F32)


def nn(a, b):
    return jnp.dot(a, b, preferred_element_type=F32)


def full(a, b):
    return jnp.dot(a, b, preferred_element_type=F32, precision=lax.Precision.HIGHEST)


def split(value):
    high = value.astype(BF16)
    return high, (value - high.astype(F32)).astype(BF16)


def reduce_kernel(
    gk, gv, ek, ev, qk, qv,
    fed, left_rows, result,
    stage, q_in, q_all, part, pair_in, ring_in, quad_in, left, share_in, shared, acc, t_plane,
    q_sem, load_sem, pair_send, pair_recv, ring_send, ring_recv, share_send, share_recv, quad_send, quad_recv,
    gather_send, gather_recv, pass_send, pass_recv, plane_send, plane_recv, last_send, last_recv,
):
    dp = lax.axis_index("dp")
    z = lax.axis_index("tensor")
    core = dp & 1
    chip = dp >> 1
    x = chip >> 2
    y = chip & 3
    bit = z & 1
    quad = z >> 1
    me = chip * 2 + bit
    xs = [(x + i) & 3 for i in range(4)]
    ys = [(y + i) & 3 for i in range(4)]
    bits = [bit, 1 - bit]
    partner = (chip * 2 + 1 - core, z)
    quads = [(dp, ((quad + i) & 3) * 2 + bit) for i in range(QUADS)]

    def device_at(offset):
        dx, dy, dz = offset
        return ((xs[dx] * 4 + ys[dy]) * 2 + core, quad * 2 + bits[dz])

    def block(step):
        inner = (step >= 2) & (step < 6)
        dx = jnp.where(step < 2, 2, jnp.where(inner, 1 + 2 * (step & 1), 0))
        half = jnp.where(inner, 2 - (step >> 1), 1 - (step & 1))
        return ((x + dx) & 3) * 2 + (((y >> 1) + half) & 1)

    def rows_of(b):
        return pl.ds(pl.multiple_of(b * ROWS, ROWS), ROWS)

    def slots_of(b):
        return pl.ds(b * SUB, SUB)

    def load(step, a, ref):
        rows = rows_of(block(step))
        return pltpu.make_async_copy(ref.at[0, rows], stage.at[a, rows], load_sem.at[step, a])

    def start_load(step, carry):
        for a, ref in enumerate((gk, gv, ek, ev)):
            load(step, a, ref).start()
        return carry

    q_loads = [pltpu.make_async_copy(q, q_in.at[m], q_sem.at[m]) for m, q in enumerate((qk, qv))]
    for q_load in q_loads:
        q_load.start()
    lax.fori_loop(0, 2, start_load, 0)

    barrier = pltpu.get_barrier_semaphore()
    for target in [device_at(offset) for offset in OFFSETS] + quads[1:] + [partner]:
        pl.semaphore_signal(barrier, inc=1, device_id=target, device_id_type=MESH)
    lax.fori_loop(2, SUPERS, start_load, 0)

    q_all[...] = jnp.zeros_like(q_all)
    for m in range(2):
        q_loads[m].wait()
        for part_of, piece in enumerate(split(q_in[m])):
            row = part_of * 2 * RANK + m * RANK
            q_all[row : row + RANK, m * F : (m + 1) * F] = piece

    def add_left(step, carry):
        b = block(step)
        rows = rows_of(b)
        for a, ref in enumerate((gk, gv, ek, ev)):
            load(step, a, ref).wait()
        highs, lows = [], []
        for m in range(2):
            value = stage[m, rows, :] + stage[2 + m, rows, :]
            fed[m, rows, :] = value
            high, low = split(value)
            highs.append(high)
            lows.append(low)
        high = jnp.concatenate(highs, axis=1)
        low = jnp.concatenate(lows, axis=1)
        product = nt(q_all[...], high)
        total = product[: 2 * RANK] + product[2 * RANK :] + nt(q_all[: 2 * RANK, :], low)
        for m in range(2):
            for j in range(SUB):
                part[m, b * SUB + j] = total[m * RANK : (m + 1) * RANK, j * 128 : (j + 1) * 128]
        return carry

    lax.fori_loop(0, SUPERS, add_left, 0)
    pl.semaphore_wait(barrier, len(OFFSETS) + QUADS)

    def pair_copy(step):
        at = slots_of(block(step))
        return pltpu.make_async_remote_copy(
            src_ref=part.at[1 - core, at], dst_ref=pair_in.at[at], send_sem=pair_send.at[step],
            recv_sem=pair_recv.at[step], device_id=partner, device_id_type=MESH)

    def start_pair(step, carry):
        pair_copy(step).start()
        return carry

    lax.fori_loop(0, SUPERS, start_pair, 0)

    def ring_copy(member):
        target = ((member >> 1) * 2 + core, quad * 2 + (member & 1))
        return pltpu.make_async_remote_copy(
            src_ref=part.at[core, member], dst_ref=ring_in.at[me], send_sem=ring_send,
            recv_sem=ring_recv, device_id=target, device_id_type=MESH)

    def scatter(step, kept):
        pair_copy(step).wait_recv()
        b = block(step)
        at = slots_of(b)
        part[core, at] = part[core, at] + pair_in[at]
        for dy in (1, 0):
            for dz in (1, 0):
                if (dy, dz) != (0, 0) or not kept:
                    ring_copy(b * SUB + ((y + dy) & 1) * 2 + bits[dz]).start()

    def scatter_step(step, carry):
        scatter(step, False)
        return carry

    lax.fori_loop(0, SUPERS - 1, scatter_step, 0)
    scatter(SUPERS - 1, True)
    ring_in[me] = part[core, me]

    def share_copy(step):
        rows = rows_of(block(step))
        return pltpu.make_async_remote_copy(
            src_ref=fed.at[1 - core, rows], dst_ref=share_in.at[rows], send_sem=share_send.at[step],
            recv_sem=share_recv.at[step], device_id=partner, device_id_type=MESH)

    def start_share(step, carry):
        share_copy(step).start()
        return carry

    lax.fori_loop(0, SUPERS, start_share, 0)

    def share_step(step, carry):
        share_copy(step).wait_recv()
        rows = rows_of(block(step))
        high, low = split(fed[core, rows, :] + share_in[rows, :])
        shared[rows, :F] = high
        shared[rows, F:] = low
        return carry

    lax.fori_loop(0, SUPERS, share_step, 0)
    most = pl.ds(0, CHIPS - 1)
    pltpu.make_async_copy(ring_in.at[most], ring_in.at[most], ring_recv).wait()
    quad_in[quad] = jnp.sum(ring_in[...], axis=0)

    for i in (2, 1, 3):
        pltpu.make_async_remote_copy(
            src_ref=quad_in.at[quad], dst_ref=quad_in.at[quad], send_sem=quad_send, recv_sem=quad_recv,
            device_id=quads[i], device_id_type=MESH).start()
    three = pl.ds(0, QUADS - 1)
    pltpu.make_async_copy(quad_in.at[three], quad_in.at[three], quad_recv).wait()
    left[core, me] = (quad_in[0] + quad_in[1]) + (quad_in[2] + quad_in[3])

    def gather_copy(slot, target):
        return pltpu.make_async_remote_copy(
            src_ref=left.at[core, slot], dst_ref=left.at[core, slot], send_sem=gather_send,
            recv_sem=gather_recv.at[slot], device_id=target, device_id_type=MESH)

    for offset in OFFSETS:
        gather_copy(me, device_at(offset)).start()

    def pass_copy(step, side):
        at = slots_of(block(step))
        return pltpu.make_async_remote_copy(
            src_ref=left.at[side, at], dst_ref=left.at[side, at], send_sem=pass_send.at[step],
            recv_sem=pass_recv.at[step], device_id=partner, device_id_type=MESH)

    def left_block(m, b):
        high, low = split(jnp.concatenate([left[m, b * SUB + j] for j in range(SUB)], axis=1))
        return jnp.concatenate([high, low], axis=0)

    def gather(step, kept):
        b = block(step)
        for dy in (0, 1):
            for dz in (0, 1):
                if (dy, dz) != (0, 0) or not kept:
                    gather_copy(b * SUB + ((y + dy) & 1) * 2 + bits[dz], partner).wait_recv()
        pass_copy(step, core).start()
        acc[...] += nn(left_block(core, b), shared[rows_of(b), :])

    def gather_step(i, carry):
        gather(SUPERS - 1 - i, False)
        return carry

    acc[...] = jnp.zeros_like(acc)
    gather(SUPERS - 1, True)
    lax.fori_loop(1, SUPERS, gather_step, 0)

    t_plane[chip] = acc[:RANK, :F] + (acc[RANK:, :F] + acc[:RANK, F:]) + acc[RANK:, F:]
    for dx, dy, dz in OFFSETS:
        if dz == 0:
            pltpu.make_async_remote_copy(
                src_ref=t_plane.at[chip], dst_ref=t_plane.at[chip], send_sem=plane_send, recv_sem=plane_recv,
                device_id=device_at((dx, dy, 0)), device_id_type=MESH).start()

    def gram_step(b, total):
        both = left_block(core, b)
        return total + nt(both, both)

    products = lax.fori_loop(0, SUPERS, gram_step, jnp.zeros((2 * RANK, 2 * RANK), F32))
    gram = (products[:RANK, :RANK] + products[RANK:, RANK:]) + (products[:RANK, RANK:] + products[RANK:, :RANK])
    row = lax.broadcasted_iota(jnp.int32, (RANK, RANK), 0)
    column = lax.broadcasted_iota(jnp.int32, (RANK, RANK), 1)
    unit = jnp.where(row == column, 1.0, 0.0).astype(F32)
    work = jnp.concatenate([unit, gram, jnp.zeros((RANK, 2 * RANK), F32)], axis=1)
    wide_row = lax.broadcasted_iota(jnp.int32, (RANK, 4 * RANK), 0)
    wide_column = lax.broadcasted_iota(jnp.int32, (RANK, 4 * RANK), 1)
    pivots = jnp.ones((RANK, 1), F32)
    for j in range(RANK):
        picked = work[:, RANK + j : RANK + j + 1]
        pivot = picked[j : j + 1, :]
        pivots = jnp.where(wide_row[:, :1] == j, pivot, pivots)
        work = work - jnp.where(wide_row[:, :1] > j, picked / pivot, 0.0) * work[j : j + 1, :]
    inverse = jnp.where(wide_column < RANK, work * lax.rsqrt(pivots), 0.0)
    lower = jnp.concatenate([inverse, jnp.zeros((3 * RANK, 4 * RANK), F32)], axis=0)
    upper = lower.T

    def turn_step(step, carry):
        pass_copy(step, 1 - core).wait_recv()
        b = block(step)
        for j in range(SUB):
            slot = b * SUB + j
            key_high, key_low = split(left[0, slot])
            value_high, value_low = split(left[1, slot])
            both = jnp.concatenate(
                [piece.astype(F32) for piece in (key_high, value_high, key_low, value_low)], axis=0)
            left_rows[pl.ds(pl.multiple_of(slot * 128, 128), 128), :] = both.T.astype(BF16)
        return carry

    lax.fori_loop(0, SUPERS, turn_step, 0)

    fifteen = pl.ds(0, PLANE - 1)
    pltpu.make_async_copy(t_plane.at[fifteen], t_plane.at[fifteen], plane_recv).wait()
    sums = jnp.concatenate([jnp.sum(t_plane[...], axis=0), jnp.zeros((3 * RANK, F), F32)], axis=0) * (1.0 / 32)
    right = full(lower, sums)
    result[core, :RANK] = right[:RANK]
    result[core, RANK:] = full(upper, right)[:RANK]
    last = pltpu.make_async_remote_copy(
        src_ref=result.at[core], dst_ref=result.at[core], send_sem=last_send, recv_sem=last_recv,
        device_id=partner, device_id_type=MESH)
    last.start()

    def end_step(step, carry):
        pair_copy(step).wait_send()
        share_copy(step).wait_send()
        pass_copy(step, core).wait_send()
        return carry

    lax.fori_loop(0, SUPERS, end_step, 0)
    pltpu.make_async_copy(ring_in.at[most], ring_in.at[most], ring_send).wait()
    pltpu.make_async_copy(quad_in.at[three], quad_in.at[three], quad_send).wait()
    pltpu.make_async_copy(ring_in.at[most], ring_in.at[most], gather_send).wait()
    pltpu.make_async_copy(t_plane.at[fifteen], t_plane.at[fifteen], plane_send).wait()
    last.wait()


def error_kernel(fed, left_rows, result, right_key, right_value, new_key, new_value, wide, out, sem):
    right_key[...] = result[0, :RANK]
    right_value[...] = result[1, :RANK]
    wide[...] = jnp.zeros_like(wide)
    for m in range(2):
        for part_of, piece in enumerate(split(result[m, RANK:])):
            for again in range(2):
                row = (2 * part_of + again) * 2 * RANK + m * RANK
                wide[row : row + RANK, m * F : (m + 1) * F] = piece
    copies = []
    for b in range(SUPERS):
        rows = slice(b * ROWS, (b + 1) * ROWS)
        tall = left_rows[rows, :]
        change = nn(jnp.concatenate([tall, tall], axis=1), wide[...])
        for m, new in enumerate((new_key, new_value)):
            out[m, rows, :] = fed[m, rows, :] - change[:, m * F : (m + 1) * F]
            copy = pltpu.make_async_copy(out.at[m, rows], new.at[0, rows], sem.at[b, m])
            copy.start()
            copies.append(copy)
    for copy in copies:
        copy.wait()


def on_device(grad_key, grad_value, error_key, error_value, factor_key, factor_value):
    vmem = pl.BlockSpec(memory_space=pltpu.VMEM)
    anywhere = pl.BlockSpec(memory_space=pl.ANY)
    dma = pltpu.SemaphoreType.DMA
    fed, left_rows, result = pl.pallas_call(
        reduce_kernel,
        out_shape=(
            pltpu.VMEM((2, D, F), F32),
            pltpu.VMEM((D, 4 * RANK), BF16),
            pltpu.VMEM((2, 2 * RANK, F), F32),
        ),
        in_specs=[anywhere] * 6,
        out_specs=(vmem,) * 3,
        scratch_shapes=[
            pltpu.VMEM((4, D, F), F32),
            pltpu.VMEM((2, RANK, F), F32),
            pltpu.VMEM((4 * RANK, 2 * F), BF16),
            pltpu.VMEM((2, CHIPS, RANK, 128), F32),
            pltpu.VMEM((CHIPS, RANK, 128), F32),
            pltpu.VMEM((CHIPS, RANK, 128), F32),
            pltpu.VMEM((QUADS, RANK, 128), F32),
            pltpu.VMEM((2, CHIPS, RANK, 128), F32),
            pltpu.VMEM((D, F), F32),
            pltpu.VMEM((D, 2 * F), BF16),
            pltpu.VMEM((2 * RANK, 2 * F), F32),
            pltpu.VMEM((PLANE, RANK, F), F32),
            dma((2,)),
            dma((SUPERS, 4)),
            dma((SUPERS,)),
            dma((SUPERS,)),
            dma,
            dma,
            dma((SUPERS,)),
            dma((SUPERS,)),
            dma,
            dma,
            dma,
            dma((CHIPS,)),
            dma((SUPERS,)),
            dma((SUPERS,)),
            dma,
            dma,
            dma,
            dma,
        ],
        compiler_params=pltpu.CompilerParams(
            collective_id=0, has_side_effects=True, vmem_limit_bytes=32 * 2**20
        ),
        cost_estimate=pl.CostEstimate(flops=10**9, bytes_accessed=12 * 2**20, transcendentals=0),
        name="reduce_factors",
    )(*(pltpu.with_memory_space_constraint(a, pltpu.HBM) for a in (grad_key, grad_value, error_key, error_value, factor_key.T, factor_value.T)))
    right_key, right_value, new_key, new_value = pl.pallas_call(
        error_kernel,
        out_shape=(
            jax.ShapeDtypeStruct((RANK, F), F32),
            jax.ShapeDtypeStruct((RANK, F), F32),
            jax.ShapeDtypeStruct((1, D, F), F32),
            jax.ShapeDtypeStruct((1, D, F), F32),
        ),
        in_specs=[vmem] * 3,
        out_specs=(vmem, vmem, anywhere, anywhere),
        scratch_shapes=[
            pltpu.VMEM((8 * RANK, 2 * F), BF16),
            pltpu.VMEM((2, D, F), F32),
            dma((SUPERS, 2)),
        ],
        compiler_params=pltpu.CompilerParams(vmem_limit_bytes=32 * 2**20),
        cost_estimate=pl.CostEstimate(flops=10**9, bytes_accessed=8 * 2**20, transcendentals=0),
        name="new_errors",
    )(fed, left_rows, result)
    return right_key.T, right_value.T, new_key, new_value


def solution(mesh):
    in_specs = (
        P("dp", None, "tensor"),
        P("dp", None, "tensor"),
        P("dp", None, "tensor"),
        P("dp", None, "tensor"),
        P("tensor", None),
        P("tensor", None),
    )
    out_specs = (
        P("tensor", None),
        P("tensor", None),
        P("dp", None, "tensor"),
        P("dp", None, "tensor"),
    )
    return jax.shard_map(
        on_device, mesh=mesh, in_specs=in_specs, out_specs=out_specs, check_vma=False
    )
```

```python
import functools

import jax
import jax.numpy as jnp
from jax import lax
from jax.experimental import pallas as pl
from jax.experimental.pallas import tpu as pltpu
from jax.sharding import PartitionSpec as P

MESH = pl.DeviceIdType.MESH
F32 = jnp.float32
BF16 = jnp.bfloat16
D = 4096
F = 128
RANK = 32
SUPERS = 8
ROWS = D // SUPERS
SUB = ROWS // 128
AHEAD = 5
CHIPS = 32
PLANE = 16
QUADS = 4


def far_first():
    offsets = [(dx, dy, dz) for dx in range(4) for dy in range(4) for dz in range(2) if dx + dy + dz > 0]
    offsets.sort(key=lambda o: -(min(o[0], 4 - o[0]) + min(o[1], 4 - o[1]) + o[2]))
    order = []
    for dx, dy, dz in offsets:
        for offset in ((dx, dy, dz), (-dx % 4, -dy % 4, dz)):
            if offset not in order:
                order.append(offset)
    return order


OFFSETS = far_first()


def nt(a, b):
    return lax.dot_general(a, b, (((1,), (1,)), ((), ())), preferred_element_type=F32)


def nn(a, b):
    return jnp.dot(a, b, preferred_element_type=F32)


def full(a, b):
    return jnp.dot(a, b, preferred_element_type=F32, precision=lax.Precision.HIGHEST)


def split(value):
    high = value.astype(BF16)
    return high, (value - high.astype(F32)).astype(BF16)


def thirds(value):
    high = value.astype(BF16)
    rest = value - high.astype(F32)
    mid = rest.astype(BF16)
    return high, mid, (rest - mid.astype(F32)).astype(BF16)


def tall_of(block):
    high, low = split(block)
    return jnp.concatenate([high.astype(F32), low.astype(F32)], axis=0).T.astype(BF16)


def wide_of(weight):
    high, low = split(weight)
    return jnp.concatenate([high, high, low, low], axis=0)


def low_rank(tall, wide):
    return nn(tall, wide[: 2 * RANK, :]) + nn(tall, wide[2 * RANK :, :])


def reduce_kernel(
    gk, gv, ek, ev, qk, qv,
    fed, left, result,
    stage, q_in, q_all, part, pair_in, ring_in, quad_in, share_in, shared, acc, gram_acc, t_plane, left_rows, own, spread,
    q_sem, load_sem, pair_send, pair_recv, ring_send, ring_recv, share_send, share_recv, quad_send, quad_recv,
    gather_send, gather_recv, pass_send, pass_recv, plane_send, plane_recv, last_send, last_recv,
):
    dp = lax.axis_index("dp")
    z = lax.axis_index("tensor")
    core = dp & 1
    chip = dp >> 1
    x = chip >> 2
    y = chip & 3
    bit = z & 1
    quad = z >> 1
    me = chip * 2 + bit
    xs = [(x + i) & 3 for i in range(4)]
    ys = [(y + i) & 3 for i in range(4)]
    bits = [bit, 1 - bit]
    partner = (chip * 2 + 1 - core, z)
    quads = [(dp, ((quad + i) & 3) * 2 + bit) for i in range(QUADS)]

    def device_at(offset):
        dx, dy, dz = offset
        return ((xs[dx] * 4 + ys[dy]) * 2 + core, quad * 2 + bits[dz])

    def block(step):
        inner = (step >= 2) & (step < 6)
        dx = jnp.where(step < 2, 2, jnp.where(inner, 1 + 2 * (step & 1), 0))
        half = jnp.where(inner, 2 - (step >> 1), 1 - (step & 1))
        return ((x + dx) & 3) * 2 + (((y >> 1) + half) & 1)

    def rows_of(b):
        return pl.ds(pl.multiple_of(b * ROWS, ROWS), ROWS)

    def slots_of(b):
        return pl.ds(b * SUB, SUB)

    def load(step, a, ref):
        rows = rows_of(block(step))
        return pltpu.make_async_copy(ref.at[0, rows], stage.at[a, rows], load_sem.at[step, a])

    def start_load(step, carry):
        for a, ref in enumerate((gk, gv, ek, ev)):
            load(step, a, ref).start()
        return carry

    q_loads = [pltpu.make_async_copy(q, q_in.at[m], q_sem.at[m]) for m, q in enumerate((qk, qv))]
    for q_load in q_loads:
        q_load.start()
    lax.fori_loop(0, 2, start_load, 0)

    barrier = pltpu.get_barrier_semaphore()
    for target in [device_at(offset) for offset in OFFSETS] + quads[1:] + [partner]:
        pl.semaphore_signal(barrier, inc=1, device_id=target, device_id_type=MESH)
    lax.fori_loop(2, SUPERS, start_load, 0)

    q_all[...] = jnp.zeros_like(q_all)
    for m in range(2):
        q_loads[m].wait()
        for part_of, piece in enumerate(split(q_in[m])):
            row = part_of * 2 * RANK + m * RANK
            q_all[row : row + RANK, m * F : (m + 1) * F] = piece

    def add_left(step, carry):
        b = block(step)
        rows = rows_of(b)
        for a, ref in enumerate((gk, gv, ek, ev)):
            load(step, a, ref).wait()
        highs, lows = [], []
        for m in range(2):
            value = stage[m, rows, :] + stage[2 + m, rows, :]
            fed[m, rows, :] = value
            high, low = split(value)
            highs.append(high)
            lows.append(low)
        high = jnp.concatenate(highs, axis=1)
        low = jnp.concatenate(lows, axis=1)
        product = nt(q_all[...], high)
        total = product[: 2 * RANK] + product[2 * RANK :] + nt(q_all[: 2 * RANK, :], low)
        for m in range(2):
            for j in range(SUB):
                part[m, b * SUB + j] = total[m * RANK : (m + 1) * RANK, j * 128 : (j + 1) * 128]
        return carry

    def pair_copy(step):
        at = slots_of(block(step))
        return pltpu.make_async_remote_copy(
            src_ref=part.at[1 - core, at], dst_ref=pair_in.at[at], send_sem=pair_send.at[step],
            recv_sem=pair_recv.at[step], device_id=partner, device_id_type=MESH)

    def ring_copy(member):
        target = ((member >> 1) * 2 + core, quad * 2 + (member & 1))
        return pltpu.make_async_remote_copy(
            src_ref=part.at[core, member], dst_ref=ring_in.at[me], send_sem=ring_send,
            recv_sem=ring_recv, device_id=target, device_id_type=MESH)

    def scatter(step, kept):
        pair_copy(step).wait_recv()
        b = block(step)
        at = slots_of(b)
        part[core, at] = part[core, at] + pair_in[at]
        for dy in (1, 0):
            for dz in (1, 0):
                if (dy, dz) != (0, 0) or not kept:
                    ring_copy(b * SUB + ((y + dy) & 1) * 2 + bits[dz]).start()

    def start_pair(step, carry):
        pair_copy(step).start()
        return carry

    def scatter_step(step, carry):
        scatter(step, False)
        return carry

    def overlapped(step, carry):
        add_left(step, 0)
        pair_copy(step).start()
        scatter(2 * (step - AHEAD), False)
        scatter(2 * (step - AHEAD) + 1, False)
        return carry

    lax.fori_loop(0, AHEAD, add_left, 0)
    pl.semaphore_wait(barrier, len(OFFSETS) + QUADS)
    lax.fori_loop(0, AHEAD, start_pair, 0)
    lax.fori_loop(AHEAD, SUPERS, overlapped, 0)
    lax.fori_loop(2 * (SUPERS - AHEAD), SUPERS - 1, scatter_step, 0)
    scatter(SUPERS - 1, True)
    ring_in[me] = part[core, me]

    def share_copy(step):
        rows = rows_of(block(step))
        return pltpu.make_async_remote_copy(
            src_ref=fed.at[1 - core, rows], dst_ref=share_in.at[rows], send_sem=share_send.at[step],
            recv_sem=share_recv.at[step], device_id=partner, device_id_type=MESH)

    def start_share(step, carry):
        share_copy(step).start()
        return carry

    lax.fori_loop(0, SUPERS, start_share, 0)

    def share_step(step, carry):
        share_copy(step).wait_recv()
        rows = rows_of(block(step))
        high, low = split(fed[core, rows, :] + share_in[rows, :])
        shared[rows, :F] = high
        shared[rows, F:] = low
        return carry

    lax.fori_loop(0, SUPERS, share_step, 0)
    most = pl.ds(0, CHIPS - 1)
    pltpu.make_async_copy(ring_in.at[most], ring_in.at[most], ring_recv).wait()
    quad_in[quad] = jnp.sum(ring_in[...], axis=0)

    for i in (2, 1, 3):
        pltpu.make_async_remote_copy(
            src_ref=quad_in.at[quad], dst_ref=quad_in.at[quad], send_sem=quad_send, recv_sem=quad_recv,
            device_id=quads[i], device_id_type=MESH).start()
    three = pl.ds(0, QUADS - 1)
    pltpu.make_async_copy(quad_in.at[three], quad_in.at[three], quad_recv).wait()
    left[core, me] = (quad_in[0] + quad_in[1]) + (quad_in[2] + quad_in[3])

    def gather_copy(slot, target):
        return pltpu.make_async_remote_copy(
            src_ref=left.at[core, slot], dst_ref=left.at[core, slot], send_sem=gather_send,
            recv_sem=gather_recv.at[slot], device_id=target, device_id_type=MESH)

    for offset in OFFSETS:
        gather_copy(me, device_at(offset)).start()

    def pass_copy(step, side):
        at = slots_of(block(step))
        return pltpu.make_async_remote_copy(
            src_ref=left.at[side, at], dst_ref=left.at[side, at], send_sem=pass_send.at[step],
            recv_sem=pass_recv.at[step], device_id=partner, device_id_type=MESH)

    def left_block(m, b):
        high, low = split(jnp.concatenate([left[m, b * SUB + j] for j in range(SUB)], axis=1))
        return jnp.concatenate([high, low], axis=0)

    def gather(step, kept):
        b = block(step)
        for dy in (0, 1):
            for dz in (0, 1):
                if (dy, dz) != (0, 0) or not kept:
                    gather_copy(b * SUB + ((y + dy) & 1) * 2 + bits[dz], partner).wait_recv()
        acc[...] += nn(left_block(core, b), shared[rows_of(b), :])

    def digest(step):
        b = block(step)
        both = left_block(core, b)
        gram_acc[...] += nt(both, both)
        for j in range(SUB):
            rows = pl.ds(pl.multiple_of((b * SUB + j) * 128, 128), 128)
            left_rows[rows, : 2 * RANK] = tall_of(left[core, b * SUB + j])

    def gather_step(step, carry):
        gather(step, False)
        return carry

    acc[...] = jnp.zeros_like(acc)
    gram_acc[...] = jnp.zeros_like(gram_acc)
    gather(0, False)
    lax.fori_loop(1, SUPERS - 1, gather_step, 0)
    gather(SUPERS - 1, True)

    t_plane[chip] = acc[:RANK, :F] + (acc[RANK:, :F] + acc[:RANK, F:]) + acc[RANK:, F:]
    for dx, dy, dz in OFFSETS:
        if dz == 0:
            pltpu.make_async_remote_copy(
                src_ref=t_plane.at[chip], dst_ref=t_plane.at[chip], send_sem=plane_send, recv_sem=plane_recv,
                device_id=device_at((dx, dy, 0)), device_id_type=MESH).start()

    def start_pass(step, carry):
        pass_copy(step, core).start()
        return carry

    lax.fori_loop(0, SUPERS, start_pass, 0)

    def digest_step(step, carry):
        digest(step)
        return carry

    lax.fori_loop(0, SUPERS, digest_step, 0)
    products = gram_acc[...]
    gram = (products[:RANK, :RANK] + products[RANK:, RANK:]) + (products[:RANK, RANK:] + products[RANK:, :RANK])
    row = lax.broadcasted_iota(jnp.int32, (RANK, RANK), 0)
    column = lax.broadcasted_iota(jnp.int32, (RANK, RANK), 1)
    unit = jnp.where(row == column, 1.0, 0.0).astype(F32)
    work = jnp.concatenate([unit, gram, jnp.zeros((RANK, 2 * RANK), F32)], axis=1)
    wide_row = lax.broadcasted_iota(jnp.int32, (RANK, 4 * RANK), 0)
    wide_column = lax.broadcasted_iota(jnp.int32, (RANK, 4 * RANK), 1)
    pivots = jnp.ones((RANK, 1), F32)
    for j in range(RANK):
        picked = work[:, RANK + j : RANK + j + 1]
        pivot = picked[j : j + 1, :]
        pivots = jnp.where(wide_row[:, :1] == j, pivot, pivots)
        work = work - jnp.where(wide_row[:, :1] > j, picked / pivot, 0.0) * work[j : j + 1, :]
    inverse = (work * lax.rsqrt(pivots))[:, :RANK]
    square = jnp.concatenate([inverse, jnp.zeros((RANK, 3 * RANK), F32)], axis=1)
    upper = jnp.concatenate([square, jnp.zeros((3 * RANK, 4 * RANK), F32)], axis=0).T
    solver = jnp.concatenate([inverse, full(upper[:RANK, :RANK], inverse)], axis=0) * (1.0 / 32)
    s_high, s_mid, s_low = thirds(solver)
    spread[:, : 6 * RANK] = jnp.concatenate([s_high, s_high, s_mid, s_mid, s_high, s_low], axis=1)

    fifteen = pl.ds(0, PLANE - 1)
    pltpu.make_async_copy(t_plane.at[fifteen], t_plane.at[fifteen], plane_recv).wait()
    high, mid, low = thirds(jnp.sum(t_plane[...], axis=0))
    result[core] = nn(spread[:, : 6 * RANK], jnp.concatenate([high, mid, high, mid, low, high], axis=0))
    last = pltpu.make_async_remote_copy(
        src_ref=result.at[core], dst_ref=result.at[core], send_sem=last_send, recv_sem=last_recv,
        device_id=partner, device_id_type=MESH)
    last.start()

    own[...] = wide_of(result[core, RANK:])

    def own_step(b, carry):
        rows = rows_of(b)
        fed[core, rows, :] = fed[core, rows, :] - low_rank(left_rows[rows, : 2 * RANK], own)
        return carry

    lax.fori_loop(0, SUPERS, own_step, 0)

    def end_step(step, carry):
        pair_copy(step).wait_send()
        share_copy(step).wait_send()
        pass_copy(step, core).wait_send()
        pass_copy(step, 1 - core).wait_recv()
        return carry

    lax.fori_loop(0, SUPERS, end_step, 0)
    pltpu.make_async_copy(ring_in.at[most], ring_in.at[most], ring_send).wait()
    pltpu.make_async_copy(quad_in.at[three], quad_in.at[three], quad_send).wait()
    pltpu.make_async_copy(ring_in.at[most], ring_in.at[most], gather_send).wait()
    pltpu.make_async_copy(t_plane.at[fifteen], t_plane.at[fifteen], plane_send).wait()
    last.wait()


def error_kernel(fed, left, result, right_key, right_value, new_key, new_value, wide, out, sem):
    core = lax.axis_index("dp") & 1
    news = (new_key, new_value)

    def write(m):
        done = pltpu.make_async_copy(fed.at[1 - m], news[1 - m].at[0], sem.at[SUPERS])
        done.start()
        right_key[...] = result[0, :RANK]
        right_value[...] = result[1, :RANK]
        wide[...] = wide_of(result[m, RANK:])
        copies = []
        for b in range(SUPERS):
            rows = slice(b * ROWS, (b + 1) * ROWS)
            tall = jnp.concatenate([tall_of(left[m, b * SUB + j]) for j in range(SUB)], axis=0)
            out[rows, :] = fed[m, rows, :] - low_rank(tall, wide)
            copies.append(pltpu.make_async_copy(out.at[rows], news[m].at[0, rows], sem.at[b]))
            copies[-1].start()
        for copy in copies:
            copy.wait()
        done.wait()

    for m in range(2):
        pl.when(core == 1 - m)(functools.partial(write, m))


def on_device(grad_key, grad_value, error_key, error_value, factor_key, factor_value):
    vmem = pl.BlockSpec(memory_space=pltpu.VMEM)
    anywhere = pl.BlockSpec(memory_space=pl.ANY)
    dma = pltpu.SemaphoreType.DMA
    fed, left, result = pl.pallas_call(
        reduce_kernel,
        out_shape=(
            pltpu.VMEM((2, D, F), F32),
            pltpu.VMEM((2, CHIPS, RANK, 128), F32),
            pltpu.VMEM((2, 2 * RANK, F), F32),
        ),
        in_specs=[anywhere] * 6,
        out_specs=(vmem,) * 3,
        scratch_shapes=[
            pltpu.VMEM((4, D, F), F32),
            pltpu.VMEM((2, RANK, F), F32),
            pltpu.VMEM((4 * RANK, 2 * F), BF16),
            pltpu.VMEM((2, CHIPS, RANK, 128), F32),
            pltpu.VMEM((CHIPS, RANK, 128), F32),
            pltpu.VMEM((CHIPS, RANK, 128), F32),
            pltpu.VMEM((QUADS, RANK, 128), F32),
            pltpu.VMEM((D, F), F32),
            pltpu.VMEM((D, 2 * F), BF16),
            pltpu.VMEM((2 * RANK, 2 * F), F32),
            pltpu.VMEM((2 * RANK, 2 * RANK), F32),
            pltpu.VMEM((PLANE, RANK, F), F32),
            pltpu.VMEM((D, 4 * RANK), BF16),
            pltpu.VMEM((4 * RANK, F), BF16),
            pltpu.VMEM((2 * RANK, 8 * RANK), BF16),
            dma((2,)),
            dma((SUPERS, 4)),
            dma((SUPERS,)),
            dma((SUPERS,)),
            dma,
            dma,
            dma((SUPERS,)),
            dma((SUPERS,)),
            dma,
            dma,
            dma,
            dma((CHIPS,)),
            dma((SUPERS,)),
            dma((SUPERS,)),
            dma,
            dma,
            dma,
            dma,
        ],
        compiler_params=pltpu.CompilerParams(
            collective_id=0, has_side_effects=True, vmem_limit_bytes=32 * 2**20
        ),
        cost_estimate=pl.CostEstimate(flops=10**9, bytes_accessed=12 * 2**20, transcendentals=0),
        name="reduce_factors",
    )(*(pltpu.with_memory_space_constraint(a, pltpu.HBM) for a in (grad_key, grad_value, error_key, error_value, factor_key.T, factor_value.T)))
    right_key, right_value, new_key, new_value = pl.pallas_call(
        error_kernel,
        out_shape=(
            jax.ShapeDtypeStruct((RANK, F), F32),
            jax.ShapeDtypeStruct((RANK, F), F32),
            jax.ShapeDtypeStruct((1, D, F), F32),
            jax.ShapeDtypeStruct((1, D, F), F32),
        ),
        in_specs=[vmem] * 3,
        out_specs=(vmem, vmem, anywhere, anywhere),
        scratch_shapes=[
            pltpu.VMEM((4 * RANK, F), BF16),
            pltpu.VMEM((D, F), F32),
            dma((SUPERS + 1,)),
        ],
        compiler_params=pltpu.CompilerParams(vmem_limit_bytes=32 * 2**20),
        cost_estimate=pl.CostEstimate(flops=10**9, bytes_accessed=8 * 2**20, transcendentals=0),
        name="new_errors",
    )(fed, left, result)
    return right_key.T, right_value.T, new_key, new_value


def solution(mesh):
    in_specs = (
        P("dp", None, "tensor"),
        P("dp", None, "tensor"),
        P("dp", None, "tensor"),
        P("dp", None, "tensor"),
        P("tensor", None),
        P("tensor", None),
    )
    out_specs = (
        P("tensor", None),
        P("tensor", None),
        P("dp", None, "tensor"),
        P("dp", None, "tensor"),
    )
    return jax.shard_map(
        on_device, mesh=mesh, in_specs=in_specs, out_specs=out_specs, check_vma=False
    )
```

```python
import functools

import jax
import jax.numpy as jnp
from jax import lax
from jax.experimental import pallas as pl
from jax.experimental.pallas import tpu as pltpu
from jax.sharding import PartitionSpec as P

MESH = pl.DeviceIdType.MESH
F32 = jnp.float32
BF16 = jnp.bfloat16
D = 4096
F = 128
RANK = 32
SUPERS = 8
ROWS = D // SUPERS
SUB = ROWS // 128
AHEAD = 5
CHIPS = 32
PLANE = 16
QUADS = 4


def far_first():
    offsets = [(dx, dy, dz) for dx in range(4) for dy in range(4) for dz in range(2) if dx + dy + dz > 0]
    offsets.sort(key=lambda o: -(min(o[0], 4 - o[0]) + min(o[1], 4 - o[1]) + o[2]))
    order = []
    for dx, dy, dz in offsets:
        for offset in ((dx, dy, dz), (-dx % 4, -dy % 4, dz)):
            if offset not in order:
                order.append(offset)
    return order


OFFSETS = far_first()


def nt(a, b):
    return lax.dot_general(a, b, (((1,), (1,)), ((), ())), preferred_element_type=F32)


def nn(a, b):
    return jnp.dot(a, b, preferred_element_type=F32)


def full(a, b):
    return jnp.dot(a, b, preferred_element_type=F32, precision=lax.Precision.HIGHEST)


def split(value):
    high = value.astype(BF16)
    return high, (value - high.astype(F32)).astype(BF16)


def thirds(value):
    high = value.astype(BF16)
    rest = value - high.astype(F32)
    mid = rest.astype(BF16)
    return high, mid, (rest - mid.astype(F32)).astype(BF16)


def tall_of(block):
    high, low = split(block)
    return jnp.concatenate([high.astype(F32), low.astype(F32)], axis=0).T.astype(BF16)


def wide_of(weight):
    high, low = split(weight)
    return jnp.concatenate([high, high, low, low], axis=0)


def low_rank(tall, wide):
    return nn(tall, wide[: 2 * RANK, :]) + nn(tall, wide[2 * RANK :, :])


def reduce_kernel(
    gk, gv, ek, ev, qk, qv,
    fed, left, result,
    stage, q_in, q_all, part, pair_in, ring_in, quad_in, share_in, shared, acc, gram_acc, t_plane, left_rows, own, spread,
    q_sem, load_sem, pair_send, pair_recv, ring_send, ring_recv, share_send, share_recv, quad_send, quad_recv,
    gather_send, gather_recv, pass_send, pass_recv, plane_send, plane_recv, last_send, last_recv,
):
    dp = lax.axis_index("dp")
    z = lax.axis_index("tensor")
    core = dp & 1
    chip = dp >> 1
    x = chip >> 2
    y = chip & 3
    shifted = (z + 8 - core) & 7
    bit = shifted & 1
    quad = shifted >> 1
    me = chip * 2 + bit
    xs = [(x + i) & 3 for i in range(4)]
    ys = [(y + i) & 3 for i in range(4)]
    bits = [bit, 1 - bit]
    partner = (chip * 2 + 1 - core, z)
    quads = [(dp, (z + 2 * i) & 7) for i in range(QUADS)]

    def device_at(offset):
        dx, dy, dz = offset
        return ((xs[dx] * 4 + ys[dy]) * 2 + core, (quad * 2 + bits[dz] + core) & 7)

    def block(step):
        inner = (step >= 2) & (step < 6)
        dx = jnp.where(step < 2, 2, jnp.where(inner, 1 + 2 * (step & 1), 0))
        half = jnp.where(inner, 2 - (step >> 1), 1 - (step & 1))
        return ((x + dx) & 3) * 2 + (((y >> 1) + half) & 1)

    def rows_of(b):
        return pl.ds(pl.multiple_of(b * ROWS, ROWS), ROWS)

    def slots_of(b):
        return pl.ds(b * SUB, SUB)

    def load(step, a, ref):
        rows = rows_of(block(step))
        return pltpu.make_async_copy(ref.at[0, rows], stage.at[a, rows], load_sem.at[step, a])

    def start_load(step, carry):
        for a, ref in enumerate((gk, gv, ek, ev)):
            load(step, a, ref).start()
        return carry

    q_loads = [pltpu.make_async_copy(q, q_in.at[m], q_sem.at[m]) for m, q in enumerate((qk, qv))]
    for q_load in q_loads:
        q_load.start()
    lax.fori_loop(0, 2, start_load, 0)

    barrier = pltpu.get_barrier_semaphore()
    for target in [device_at(offset) for offset in OFFSETS] + quads[1:] + [partner]:
        pl.semaphore_signal(barrier, inc=1, device_id=target, device_id_type=MESH)
    lax.fori_loop(2, SUPERS, start_load, 0)

    q_all[...] = jnp.zeros_like(q_all)
    for m in range(2):
        q_loads[m].wait()
        for part_of, piece in enumerate(split(q_in[m])):
            row = part_of * 2 * RANK + m * RANK
            q_all[row : row + RANK, m * F : (m + 1) * F] = piece

    def add_left(step, carry):
        b = block(step)
        rows = rows_of(b)
        for a, ref in enumerate((gk, gv, ek, ev)):
            load(step, a, ref).wait()
        highs, lows = [], []
        for m in range(2):
            value = stage[m, rows, :] + stage[2 + m, rows, :]
            fed[m, rows, :] = value
            high, low = split(value)
            highs.append(high)
            lows.append(low)
        high = jnp.concatenate(highs, axis=1)
        low = jnp.concatenate(lows, axis=1)
        product = nt(q_all[...], high)
        total = product[: 2 * RANK] + product[2 * RANK :] + nt(q_all[: 2 * RANK, :], low)
        for m in range(2):
            for j in range(SUB):
                part[m, b * SUB + j] = total[m * RANK : (m + 1) * RANK, j * 128 : (j + 1) * 128]
        return carry

    def pair_copy(step):
        at = slots_of(block(step))
        return pltpu.make_async_remote_copy(
            src_ref=part.at[1 - core, at], dst_ref=pair_in.at[at], send_sem=pair_send,
            recv_sem=pair_recv.at[step], device_id=partner, device_id_type=MESH)

    def ring_copy(member):
        target = ((member >> 1) * 2 + core, (quad * 2 + (member & 1) + core) & 7)
        return pltpu.make_async_remote_copy(
            src_ref=part.at[core, member], dst_ref=ring_in.at[me], send_sem=ring_send,
            recv_sem=ring_recv, device_id=target, device_id_type=MESH)

    def scatter(step, kept):
        pair_copy(step).wait_recv()
        b = block(step)
        at = slots_of(b)
        part[core, at] = part[core, at] + pair_in[at]
        for dy in (1, 0):
            for dz in (1, 0):
                if (dy, dz) != (0, 0) or not kept:
                    ring_copy(b * SUB + ((y + dy) & 1) * 2 + bits[dz]).start()

    def start_pair(step, carry):
        pair_copy(step).start()
        return carry

    def scatter_step(step, carry):
        scatter(step, False)
        return carry

    def overlapped(step, carry):
        add_left(step, 0)
        pair_copy(step).start()
        scatter(2 * (step - AHEAD), False)
        scatter(2 * (step - AHEAD) + 1, False)
        return carry

    lax.fori_loop(0, AHEAD, add_left, 0)
    pl.semaphore_wait(barrier, len(OFFSETS) + QUADS)
    lax.fori_loop(0, AHEAD, start_pair, 0)
    lax.fori_loop(AHEAD, SUPERS, overlapped, 0)
    lax.fori_loop(2 * (SUPERS - AHEAD), SUPERS - 1, scatter_step, 0)
    scatter(SUPERS - 1, True)
    ring_in[me] = part[core, me]

    def share_copy(step):
        rows = rows_of(block(step))
        return pltpu.make_async_remote_copy(
            src_ref=fed.at[1 - core, rows], dst_ref=share_in.at[rows], send_sem=share_send,
            recv_sem=share_recv.at[step], device_id=partner, device_id_type=MESH)

    def start_share(step, carry):
        share_copy(step).start()
        return carry

    lax.fori_loop(0, SUPERS, start_share, 0)

    def share_step(step, carry):
        share_copy(step).wait_recv()
        rows = rows_of(block(step))
        high, low = split(fed[core, rows, :] + share_in[rows, :])
        shared[rows, :F] = high
        shared[rows, F:] = low
        return carry

    lax.fori_loop(0, SUPERS, share_step, 0)
    most = pl.ds(0, CHIPS - 1)
    pltpu.make_async_copy(ring_in.at[most], ring_in.at[most], ring_recv).wait()
    quad_in[quad] = jnp.sum(ring_in[...], axis=0)

    for i in (2, 1, 3):
        pltpu.make_async_remote_copy(
            src_ref=quad_in.at[quad], dst_ref=quad_in.at[quad], send_sem=quad_send, recv_sem=quad_recv,
            device_id=quads[i], device_id_type=MESH).start()
    three = pl.ds(0, QUADS - 1)
    pltpu.make_async_copy(quad_in.at[three], quad_in.at[three], quad_recv).wait()
    left[core, me] = (quad_in[0] + quad_in[1]) + (quad_in[2] + quad_in[3])

    for offset in OFFSETS:
        pltpu.make_async_remote_copy(
            src_ref=left.at[core, me], dst_ref=left.at[core, me], send_sem=gather_send,
            recv_sem=gather_recv.at[chip >> 1], device_id=device_at(offset), device_id_type=MESH).start()

    def pass_copy(step, side):
        at = slots_of(block(step))
        return pltpu.make_async_remote_copy(
            src_ref=left.at[side, at], dst_ref=left.at[side, at], send_sem=pass_send,
            recv_sem=pass_recv, device_id=partner, device_id_type=MESH)

    def left_block(m, b):
        high, low = split(jnp.concatenate([left[m, b * SUB + j] for j in range(SUB)], axis=1))
        return jnp.concatenate([high, low], axis=0)

    def gather(step, kept):
        b = block(step)
        arrived = left.at[core, pl.ds(b * SUB, SUB - 1 if kept else SUB)]
        pltpu.make_async_copy(arrived, arrived, gather_recv.at[b]).wait()
        acc[...] += nn(left_block(core, b), shared[rows_of(b), :])

    def digest(step):
        b = block(step)
        both = left_block(core, b)
        gram_acc[...] += nt(both, both)
        for j in range(SUB):
            rows = pl.ds(pl.multiple_of((b * SUB + j) * 128, 128), 128)
            left_rows[rows, : 2 * RANK] = tall_of(left[core, b * SUB + j])

    def gather_step(step, carry):
        gather(step, False)
        return carry

    acc[...] = jnp.zeros_like(acc)
    gram_acc[...] = jnp.zeros_like(gram_acc)
    gather(0, False)
    lax.fori_loop(1, SUPERS - 1, gather_step, 0)
    gather(SUPERS - 1, True)

    t_plane[chip] = acc[:RANK, :F] + (acc[RANK:, :F] + acc[:RANK, F:]) + acc[RANK:, F:]
    for dx, dy, dz in OFFSETS:
        if dz == 0:
            pltpu.make_async_remote_copy(
                src_ref=t_plane.at[chip], dst_ref=t_plane.at[chip], send_sem=plane_send, recv_sem=plane_recv,
                device_id=device_at((dx, dy, 0)), device_id_type=MESH).start()

    def start_pass(step, carry):
        pass_copy(step, core).start()
        return carry

    lax.fori_loop(0, SUPERS, start_pass, 0)

    def digest_step(step, carry):
        digest(step)
        return carry

    lax.fori_loop(0, SUPERS, digest_step, 0)
    products = gram_acc[...]
    gram = (products[:RANK, :RANK] + products[RANK:, RANK:]) + (products[:RANK, RANK:] + products[RANK:, :RANK])
    row = lax.broadcasted_iota(jnp.int32, (RANK, RANK), 0)
    column = lax.broadcasted_iota(jnp.int32, (RANK, RANK), 1)
    unit = jnp.where(row == column, 1.0, 0.0).astype(F32)
    work = jnp.concatenate([unit, gram, jnp.zeros((RANK, 2 * RANK), F32)], axis=1)
    wide_row = lax.broadcasted_iota(jnp.int32, (RANK, 4 * RANK), 0)
    wide_column = lax.broadcasted_iota(jnp.int32, (RANK, 4 * RANK), 1)
    pivots = jnp.ones((RANK, 1), F32)
    for j in range(RANK):
        picked = work[:, RANK + j : RANK + j + 1]
        pivot = picked[j : j + 1, :]
        pivots = jnp.where(wide_row[:, :1] == j, pivot, pivots)
        work = work - jnp.where(wide_row[:, :1] > j, picked / pivot, 0.0) * work[j : j + 1, :]
    inverse = (work * lax.rsqrt(pivots))[:, :RANK]
    square = jnp.concatenate([inverse, jnp.zeros((RANK, 3 * RANK), F32)], axis=1)
    upper = jnp.concatenate([square, jnp.zeros((3 * RANK, 4 * RANK), F32)], axis=0).T
    solver = jnp.concatenate([inverse, full(upper[:RANK, :RANK], inverse)], axis=0) * (1.0 / 32)
    s_high, s_mid, s_low = thirds(solver)
    spread[:, : 6 * RANK] = jnp.concatenate([s_high, s_high, s_mid, s_mid, s_high, s_low], axis=1)

    fifteen = pl.ds(0, PLANE - 1)
    pltpu.make_async_copy(t_plane.at[fifteen], t_plane.at[fifteen], plane_recv).wait()
    high, mid, low = thirds(jnp.sum(t_plane[...], axis=0))
    result[core] = nn(spread[:, : 6 * RANK], jnp.concatenate([high, mid, high, mid, low, high], axis=0))
    last = pltpu.make_async_remote_copy(
        src_ref=result.at[core], dst_ref=result.at[core], send_sem=last_send, recv_sem=last_recv,
        device_id=partner, device_id_type=MESH)
    last.start()

    own[...] = wide_of(result[core, RANK:])

    def own_step(b, carry):
        rows = rows_of(b)
        fed[core, rows, :] = fed[core, rows, :] - low_rank(left_rows[rows, : 2 * RANK], own)
        return carry

    lax.fori_loop(0, SUPERS, own_step, 0)

    for ref, sem in ((pair_in, pair_send), (share_in, share_send), (ring_in, pass_send), (ring_in, pass_recv)):
        pltpu.make_async_copy(ref, ref, sem).wait()
    pltpu.make_async_copy(ring_in.at[most], ring_in.at[most], ring_send).wait()
    pltpu.make_async_copy(quad_in.at[three], quad_in.at[three], quad_send).wait()
    pltpu.make_async_copy(ring_in.at[most], ring_in.at[most], gather_send).wait()
    pltpu.make_async_copy(t_plane.at[fifteen], t_plane.at[fifteen], plane_send).wait()
    last.wait()


def error_kernel(fed, left, result, right_key, right_value, new_key, new_value, wide, out, sem):
    core = lax.axis_index("dp") & 1
    news = (new_key, new_value)

    def write(m):
        done = pltpu.make_async_copy(fed.at[1 - m], news[1 - m].at[0], sem.at[SUPERS])
        done.start()
        right_key[...] = result[0, :RANK]
        right_value[...] = result[1, :RANK]
        wide[...] = wide_of(result[m, RANK:])
        copies = []
        for b in range(SUPERS):
            rows = slice(b * ROWS, (b + 1) * ROWS)
            tall = jnp.concatenate([tall_of(left[m, b * SUB + j]) for j in range(SUB)], axis=0)
            out[rows, :] = fed[m, rows, :] - low_rank(tall, wide)
            copies.append(pltpu.make_async_copy(out.at[rows], news[m].at[0, rows], sem.at[b]))
            copies[-1].start()
        for copy in copies:
            copy.wait()
        done.wait()

    for m in range(2):
        pl.when(core == 1 - m)(functools.partial(write, m))


def on_device(grad_key, grad_value, error_key, error_value, factor_key, factor_value):
    vmem = pl.BlockSpec(memory_space=pltpu.VMEM)
    anywhere = pl.BlockSpec(memory_space=pl.ANY)
    dma = pltpu.SemaphoreType.DMA
    fed, left, result = pl.pallas_call(
        reduce_kernel,
        out_shape=(
            pltpu.VMEM((2, D, F), F32),
            pltpu.VMEM((2, CHIPS, RANK, 128), F32),
            pltpu.VMEM((2, 2 * RANK, F), F32),
        ),
        in_specs=[anywhere] * 6,
        out_specs=(vmem,) * 3,
        scratch_shapes=[
            pltpu.VMEM((4, D, F), F32),
            pltpu.VMEM((2, RANK, F), F32),
            pltpu.VMEM((4 * RANK, 2 * F), BF16),
            pltpu.VMEM((2, CHIPS, RANK, 128), F32),
            pltpu.VMEM((CHIPS, RANK, 128), F32),
            pltpu.VMEM((CHIPS, RANK, 128), F32),
            pltpu.VMEM((QUADS, RANK, 128), F32),
            pltpu.VMEM((D, F), F32),
            pltpu.VMEM((D, 2 * F), BF16),
            pltpu.VMEM((2 * RANK, 2 * F), F32),
            pltpu.VMEM((2 * RANK, 2 * RANK), F32),
            pltpu.VMEM((PLANE, RANK, F), F32),
            pltpu.VMEM((D, 4 * RANK), BF16),
            pltpu.VMEM((4 * RANK, F), BF16),
            pltpu.VMEM((2 * RANK, 8 * RANK), BF16),
            dma((2,)),
            dma((SUPERS, 4)),
            dma,
            dma((SUPERS,)),
            dma,
            dma,
            dma,
            dma((SUPERS,)),
            dma,
            dma,
            dma,
            dma((SUPERS,)),
            dma,
            dma,
            dma,
            dma,
            dma,
            dma,
        ],
        compiler_params=pltpu.CompilerParams(
            collective_id=0, has_side_effects=True, vmem_limit_bytes=32 * 2**20
        ),
        cost_estimate=pl.CostEstimate(flops=10**9, bytes_accessed=12 * 2**20, transcendentals=0),
        name="reduce_factors",
    )(*(pltpu.with_memory_space_constraint(a, pltpu.HBM) for a in (grad_key, grad_value, error_key, error_value, factor_key.T, factor_value.T)))
    right_key, right_value, new_key, new_value = pl.pallas_call(
        error_kernel,
        out_shape=(
            jax.ShapeDtypeStruct((RANK, F), F32),
            jax.ShapeDtypeStruct((RANK, F), F32),
            jax.ShapeDtypeStruct((1, D, F), F32),
            jax.ShapeDtypeStruct((1, D, F), F32),
        ),
        in_specs=[vmem] * 3,
        out_specs=(vmem, vmem, anywhere, anywhere),
        scratch_shapes=[
            pltpu.VMEM((4 * RANK, F), BF16),
            pltpu.VMEM((D, F), F32),
            dma((SUPERS + 1,)),
        ],
        compiler_params=pltpu.CompilerParams(vmem_limit_bytes=32 * 2**20),
        cost_estimate=pl.CostEstimate(flops=10**9, bytes_accessed=8 * 2**20, transcendentals=0),
        name="new_errors",
    )(fed, left, result)
    return right_key.T, right_value.T, new_key, new_value


def solution(mesh):
    in_specs = (
        P("dp", None, "tensor"),
        P("dp", None, "tensor"),
        P("dp", None, "tensor"),
        P("dp", None, "tensor"),
        P("tensor", None),
        P("tensor", None),
    )
    out_specs = (
        P("tensor", None),
        P("tensor", None),
        P("dp", None, "tensor"),
        P("dp", None, "tensor"),
    )
    return jax.shard_map(
        on_device, mesh=mesh, in_specs=in_specs, out_specs=out_specs, check_vma=False
    )
```

```python
import functools

import jax
import jax.numpy as jnp
from jax import lax
from jax.experimental import pallas as pl
from jax.experimental.pallas import tpu as pltpu
from jax.sharding import PartitionSpec as P

MESH = pl.DeviceIdType.MESH
F32 = jnp.float32
BF16 = jnp.bfloat16
D = 4096
F = 128
RANK = 32
SUPERS = 8
ROWS = D // SUPERS
SUB = ROWS // 128
AHEAD = 5
CHIPS = 32
PLANE = 16
QUADS = 4


def far_first():
    offsets = [(dx, dy, dz) for dx in range(4) for dy in range(4) for dz in range(2) if dx + dy + dz > 0]
    offsets.sort(key=lambda o: -(min(o[0], 4 - o[0]) + min(o[1], 4 - o[1]) + o[2]))
    order = []
    for dx, dy, dz in offsets:
        for offset in ((dx, dy, dz), (-dx % 4, -dy % 4, dz)):
            if offset not in order:
                order.append(offset)
    return order


OFFSETS = far_first()


def nt(a, b):
    return lax.dot_general(a, b, (((1,), (1,)), ((), ())), preferred_element_type=F32)


def nn(a, b):
    return jnp.dot(a, b, preferred_element_type=F32)


def full(a, b):
    return jnp.dot(a, b, preferred_element_type=F32, precision=lax.Precision.HIGHEST)


def split(value):
    high = value.astype(BF16)
    return high, (value - high.astype(F32)).astype(BF16)


def thirds(value):
    high = value.astype(BF16)
    rest = value - high.astype(F32)
    mid = rest.astype(BF16)
    return high, mid, (rest - mid.astype(F32)).astype(BF16)


def tall_of(block):
    high, low = split(block)
    return jnp.concatenate([high.astype(F32), low.astype(F32)], axis=0).T.astype(BF16)


def wide_of(weight):
    high, low = split(weight)
    return jnp.concatenate([high, high, low, low], axis=0)


def low_rank(tall, wide):
    return nn(tall, wide[: 2 * RANK, :]) + nn(tall, wide[2 * RANK :, :])


def reduce_kernel(
    gk, gv, ek, ev, qk, qv,
    fed, left, result,
    stage, q_in, q_all, part, pair_in, ring_in, quad_in, share_in, shared, acc, gram_acc, t_plane, left_rows, own, spread,
    q_sem, load_sem, pair_send, pair_recv, ring_send, ring_recv, share_send, share_recv, quad_send, quad_recv,
    gather_send, gather_recv, pass_send, pass_recv, plane_send, plane_recv, last_send, last_recv,
):
    dp = lax.axis_index("dp")
    z = lax.axis_index("tensor")
    core = dp & 1
    chip = dp >> 1
    x = chip >> 2
    y = chip & 3
    shifted = (z + 8 - core) & 7
    bit = shifted & 1
    quad = shifted >> 1
    me = chip * 2 + bit
    xs = [(x + i) & 3 for i in range(4)]
    ys = [(y + i) & 3 for i in range(4)]
    bits = [bit, 1 - bit]
    partner = (chip * 2 + 1 - core, z)
    quads = [(dp, (z + 2 * i) & 7) for i in range(QUADS)]

    def device_at(offset):
        dx, dy, dz = offset
        return ((xs[dx] * 4 + ys[dy]) * 2 + core, (quad * 2 + bits[dz] + core) & 7)

    def block(step):
        inner = (step >= 2) & (step < 6)
        dx = jnp.where(step < 2, 2, jnp.where(inner, 1 + 2 * (step & 1), 0))
        half = jnp.where(inner, 2 - (step >> 1), 1 - (step & 1))
        return ((x + dx) & 3) * 2 + (((y >> 1) + half) & 1)

    def rows_of(b):
        return pl.ds(pl.multiple_of(b * ROWS, ROWS), ROWS)

    def slots_of(b):
        return pl.ds(b * SUB, SUB)

    def load(step, a, ref):
        rows = rows_of(block(step))
        return pltpu.make_async_copy(ref.at[0, rows], stage.at[a, rows], load_sem.at[step, a])

    def start_load(step, carry):
        for a, ref in enumerate((gk, gv, ek, ev)):
            load(step, a, ref).start()
        return carry

    q_loads = [pltpu.make_async_copy(q, q_in.at[m], q_sem.at[m]) for m, q in enumerate((qk, qv))]
    for q_load in q_loads:
        q_load.start()
    lax.fori_loop(0, 2, start_load, 0)

    barrier = pltpu.get_barrier_semaphore()
    for target in [device_at(offset) for offset in OFFSETS] + quads[1:] + [partner]:
        pl.semaphore_signal(barrier, inc=1, device_id=target, device_id_type=MESH)
    lax.fori_loop(2, SUPERS, start_load, 0)

    q_all[...] = jnp.zeros_like(q_all)
    for m in range(2):
        q_loads[m].wait()
        for part_of, piece in enumerate(split(q_in[m])):
            row = part_of * 2 * RANK + m * RANK
            q_all[row : row + RANK, m * F : (m + 1) * F] = piece

    def add_left(step, carry):
        b = block(step)
        rows = rows_of(b)
        for a, ref in enumerate((gk, gv, ek, ev)):
            load(step, a, ref).wait()
        highs, lows = [], []
        for m in range(2):
            value = stage[m, rows, :] + stage[2 + m, rows, :]
            fed[m, rows, :] = value
            high, low = split(value)
            highs.append(high)
            lows.append(low)
        high = jnp.concatenate(highs, axis=1)
        low = jnp.concatenate(lows, axis=1)
        product = nt(q_all[...], high)
        total = product[: 2 * RANK] + product[2 * RANK :] + nt(q_all[: 2 * RANK, :], low)
        for m in range(2):
            for j in range(SUB):
                part[m, b * SUB + j] = total[m * RANK : (m + 1) * RANK, j * 128 : (j + 1) * 128]
        return carry

    def pair_copy(step):
        at = slots_of(block(step))
        return pltpu.make_async_remote_copy(
            src_ref=part.at[1 - core, at], dst_ref=pair_in.at[at], send_sem=pair_send,
            recv_sem=pair_recv.at[step], device_id=partner, device_id_type=MESH)

    def ring_copy(member):
        target = ((member >> 1) * 2 + core, (quad * 2 + (member & 1) + core) & 7)
        return pltpu.make_async_remote_copy(
            src_ref=part.at[core, member], dst_ref=ring_in.at[me], send_sem=ring_send,
            recv_sem=ring_recv, device_id=target, device_id_type=MESH)

    def scatter(step, kept):
        pair_copy(step).wait_recv()
        b = block(step)
        at = slots_of(b)
        part[core, at] = part[core, at] + pair_in[at]
        for dy in (1, 0):
            for dz in (1, 0):
                if (dy, dz) != (0, 0) or not kept:
                    ring_copy(b * SUB + ((y + dy) & 1) * 2 + bits[dz]).start()

    def start_pair(step, carry):
        pair_copy(step).start()
        return carry

    def overlapped(step, carry):
        add_left(step, 0)
        pair_copy(step).start()
        scatter(2 * (step - AHEAD), False)
        scatter(2 * (step - AHEAD) + 1, False)
        return carry

    lax.fori_loop(0, AHEAD, add_left, 0)
    pl.semaphore_wait(barrier, len(OFFSETS) + QUADS)
    for step in range(AHEAD):
        start_pair(step, 0)
    for step in range(AHEAD, SUPERS):
        overlapped(step, 0)
    for step in range(2 * (SUPERS - AHEAD), SUPERS - 1):
        scatter(step, False)
    scatter(SUPERS - 1, True)
    ring_in[me] = part[core, me]

    def share_copy(step):
        rows = rows_of(block(step))
        return pltpu.make_async_remote_copy(
            src_ref=fed.at[1 - core, rows], dst_ref=share_in.at[rows], send_sem=share_send,
            recv_sem=share_recv.at[step], device_id=partner, device_id_type=MESH)

    def start_share(step, carry):
        share_copy(step).start()
        return carry

    lax.fori_loop(0, SUPERS, start_share, 0)

    def share_step(step, carry):
        share_copy(step).wait_recv()
        rows = rows_of(block(step))
        high, low = split(fed[core, rows, :] + share_in[rows, :])
        shared[rows, :F] = high
        shared[rows, F:] = low
        return carry

    lax.fori_loop(0, SUPERS, share_step, 0)
    most = pl.ds(0, CHIPS - 1)
    pltpu.make_async_copy(ring_in.at[most], ring_in.at[most], ring_recv).wait()
    quad_in[quad] = jnp.sum(ring_in[...], axis=0)

    for i in (2, 1, 3):
        pltpu.make_async_remote_copy(
            src_ref=quad_in.at[quad], dst_ref=quad_in.at[quad], send_sem=quad_send, recv_sem=quad_recv,
            device_id=quads[i], device_id_type=MESH).start()
    three = pl.ds(0, QUADS - 1)
    pltpu.make_async_copy(quad_in.at[three], quad_in.at[three], quad_recv).wait()
    left[core, me] = (quad_in[0] + quad_in[1]) + (quad_in[2] + quad_in[3])

    for offset in OFFSETS:
        pltpu.make_async_remote_copy(
            src_ref=left.at[core, me], dst_ref=left.at[core, me], send_sem=gather_send,
            recv_sem=gather_recv.at[chip >> 1], device_id=device_at(offset), device_id_type=MESH).start()

    def pass_copy(step, side):
        at = slots_of(block(step))
        return pltpu.make_async_remote_copy(
            src_ref=left.at[side, at], dst_ref=left.at[side, at], send_sem=pass_send,
            recv_sem=pass_recv, device_id=partner, device_id_type=MESH)

    def left_block(m, b):
        high, low = split(jnp.concatenate([left[m, b * SUB + j] for j in range(SUB)], axis=1))
        return jnp.concatenate([high, low], axis=0)

    def gather(step, kept):
        b = block(step)
        arrived = left.at[core, pl.ds(b * SUB, SUB - 1 if kept else SUB)]
        pltpu.make_async_copy(arrived, arrived, gather_recv.at[b]).wait()
        acc[...] += nn(left_block(core, b), shared[rows_of(b), :])

    def digest(step):
        b = block(step)
        both = left_block(core, b)
        gram_acc[...] += nt(both, both)
        for j in range(SUB):
            rows = pl.ds(pl.multiple_of((b * SUB + j) * 128, 128), 128)
            left_rows[rows, : 2 * RANK] = tall_of(left[core, b * SUB + j])

    def gather_step(step, carry):
        gather(step, False)
        return carry

    acc[...] = jnp.zeros_like(acc)
    gram_acc[...] = jnp.zeros_like(gram_acc)
    for step in range(SUPERS - 1):
        gather(step, False)
    gather(SUPERS - 1, True)

    t_plane[chip] = acc[:RANK, :F] + (acc[RANK:, :F] + acc[:RANK, F:]) + acc[RANK:, F:]
    for dx, dy, dz in OFFSETS:
        if dz == 0:
            pltpu.make_async_remote_copy(
                src_ref=t_plane.at[chip], dst_ref=t_plane.at[chip], send_sem=plane_send, recv_sem=plane_recv,
                device_id=device_at((dx, dy, 0)), device_id_type=MESH).start()

    def start_pass(step, carry):
        pass_copy(step, core).start()
        return carry

    lax.fori_loop(0, SUPERS, start_pass, 0)

    def digest_step(step, carry):
        digest(step)
        return carry

    lax.fori_loop(0, SUPERS, digest_step, 0)
    products = gram_acc[...]
    gram = (products[:RANK, :RANK] + products[RANK:, RANK:]) + (products[:RANK, RANK:] + products[RANK:, :RANK])
    row = lax.broadcasted_iota(jnp.int32, (RANK, RANK), 0)
    column = lax.broadcasted_iota(jnp.int32, (RANK, RANK), 1)
    unit = jnp.where(row == column, 1.0, 0.0).astype(F32)
    work = jnp.concatenate([unit, gram, jnp.zeros((RANK, 2 * RANK), F32)], axis=1)
    wide_row = lax.broadcasted_iota(jnp.int32, (RANK, 4 * RANK), 0)
    wide_column = lax.broadcasted_iota(jnp.int32, (RANK, 4 * RANK), 1)
    pivots = jnp.ones((RANK, 1), F32)
    for j in range(RANK):
        picked = work[:, RANK + j : RANK + j + 1]
        pivot = picked[j : j + 1, :]
        pivots = jnp.where(wide_row[:, :1] == j, pivot, pivots)
        work = work - jnp.where(wide_row[:, :1] > j, picked / pivot, 0.0) * work[j : j + 1, :]
    inverse = (work * lax.rsqrt(pivots))[:, :RANK]
    square = jnp.concatenate([inverse, jnp.zeros((RANK, 3 * RANK), F32)], axis=1)
    upper = jnp.concatenate([square, jnp.zeros((3 * RANK, 4 * RANK), F32)], axis=0).T
    solver = jnp.concatenate([inverse, full(upper[:RANK, :RANK], inverse)], axis=0) * (1.0 / 32)
    s_high, s_mid, s_low = thirds(solver)
    spread[:, : 6 * RANK] = jnp.concatenate([s_high, s_high, s_mid, s_mid, s_high, s_low], axis=1)

    fifteen = pl.ds(0, PLANE - 1)
    pltpu.make_async_copy(t_plane.at[fifteen], t_plane.at[fifteen], plane_recv).wait()
    high, mid, low = thirds(jnp.sum(t_plane[...], axis=0))
    result[core] = nn(spread[:, : 6 * RANK], jnp.concatenate([high, mid, high, mid, low, high], axis=0))
    last = pltpu.make_async_remote_copy(
        src_ref=result.at[core], dst_ref=result.at[core], send_sem=last_send, recv_sem=last_recv,
        device_id=partner, device_id_type=MESH)
    last.start()

    own[...] = wide_of(result[core, RANK:])

    def own_step(b, carry):
        rows = rows_of(b)
        fed[core, rows, :] = fed[core, rows, :] - low_rank(left_rows[rows, : 2 * RANK], own)
        return carry

    lax.fori_loop(0, SUPERS, own_step, 0)

    for ref, sem in ((pair_in, pair_send), (share_in, share_send), (ring_in, pass_send), (ring_in, pass_recv)):
        pltpu.make_async_copy(ref, ref, sem).wait()
    pltpu.make_async_copy(ring_in.at[most], ring_in.at[most], ring_send).wait()
    pltpu.make_async_copy(quad_in.at[three], quad_in.at[three], quad_send).wait()
    pltpu.make_async_copy(ring_in.at[most], ring_in.at[most], gather_send).wait()
    pltpu.make_async_copy(t_plane.at[fifteen], t_plane.at[fifteen], plane_send).wait()
    last.wait()


def error_kernel(fed, left, result, right_key, right_value, new_key, new_value, wide, out, sem):
    core = lax.axis_index("dp") & 1
    news = (new_key, new_value)

    def write(m):
        done = pltpu.make_async_copy(fed.at[1 - m], news[1 - m].at[0], sem.at[SUPERS])
        done.start()
        right_key[...] = result[0, :RANK]
        right_value[...] = result[1, :RANK]
        wide[...] = wide_of(result[m, RANK:])
        copies = []
        for b in range(SUPERS):
            rows = slice(b * ROWS, (b + 1) * ROWS)
            tall = jnp.concatenate([tall_of(left[m, b * SUB + j]) for j in range(SUB)], axis=0)
            out[rows, :] = fed[m, rows, :] - low_rank(tall, wide)
            copies.append(pltpu.make_async_copy(out.at[rows], news[m].at[0, rows], sem.at[b]))
            copies[-1].start()
        for copy in copies:
            copy.wait()
        done.wait()

    for m in range(2):
        pl.when(core == 1 - m)(functools.partial(write, m))


def on_device(grad_key, grad_value, error_key, error_value, factor_key, factor_value):
    vmem = pl.BlockSpec(memory_space=pltpu.VMEM)
    anywhere = pl.BlockSpec(memory_space=pl.ANY)
    dma = pltpu.SemaphoreType.DMA
    fed, left, result = pl.pallas_call(
        reduce_kernel,
        out_shape=(
            pltpu.VMEM((2, D, F), F32),
            pltpu.VMEM((2, CHIPS, RANK, 128), F32),
            pltpu.VMEM((2, 2 * RANK, F), F32),
        ),
        in_specs=[anywhere] * 6,
        out_specs=(vmem,) * 3,
        scratch_shapes=[
            pltpu.VMEM((4, D, F), F32),
            pltpu.VMEM((2, RANK, F), F32),
            pltpu.VMEM((4 * RANK, 2 * F), BF16),
            pltpu.VMEM((2, CHIPS, RANK, 128), F32),
            pltpu.VMEM((CHIPS, RANK, 128), F32),
            pltpu.VMEM((CHIPS, RANK, 128), F32),
            pltpu.VMEM((QUADS, RANK, 128), F32),
            pltpu.VMEM((D, F), F32),
            pltpu.VMEM((D, 2 * F), BF16),
            pltpu.VMEM((2 * RANK, 2 * F), F32),
            pltpu.VMEM((2 * RANK, 2 * RANK), F32),
            pltpu.VMEM((PLANE, RANK, F), F32),
            pltpu.VMEM((D, 4 * RANK), BF16),
            pltpu.VMEM((4 * RANK, F), BF16),
            pltpu.VMEM((2 * RANK, 8 * RANK), BF16),
            dma((2,)),
            dma((SUPERS, 4)),
            dma,
            dma((SUPERS,)),
            dma,
            dma,
            dma,
            dma((SUPERS,)),
            dma,
            dma,
            dma,
            dma((SUPERS,)),
            dma,
            dma,
            dma,
            dma,
            dma,
            dma,
        ],
        compiler_params=pltpu.CompilerParams(
            collective_id=0, has_side_effects=True, vmem_limit_bytes=32 * 2**20
        ),
        cost_estimate=pl.CostEstimate(flops=10**9, bytes_accessed=12 * 2**20, transcendentals=0),
        name="reduce_factors",
    )(*(pltpu.with_memory_space_constraint(a, pltpu.HBM) for a in (grad_key, grad_value, error_key, error_value, factor_key.T, factor_value.T)))
    right_key, right_value, new_key, new_value = pl.pallas_call(
        error_kernel,
        out_shape=(
            jax.ShapeDtypeStruct((RANK, F), F32),
            jax.ShapeDtypeStruct((RANK, F), F32),
            jax.ShapeDtypeStruct((1, D, F), F32),
            jax.ShapeDtypeStruct((1, D, F), F32),
        ),
        in_specs=[vmem] * 3,
        out_specs=(vmem, vmem, anywhere, anywhere),
        scratch_shapes=[
            pltpu.VMEM((4 * RANK, F), BF16),
            pltpu.VMEM((D, F), F32),
            dma((SUPERS + 1,)),
        ],
        compiler_params=pltpu.CompilerParams(vmem_limit_bytes=32 * 2**20),
        cost_estimate=pl.CostEstimate(flops=10**9, bytes_accessed=8 * 2**20, transcendentals=0),
        name="new_errors",
    )(fed, left, result)
    return right_key.T, right_value.T, new_key, new_value


def solution(mesh):
    in_specs = (
        P("dp", None, "tensor"),
        P("dp", None, "tensor"),
        P("dp", None, "tensor"),
        P("dp", None, "tensor"),
        P("tensor", None),
        P("tensor", None),
    )
    out_specs = (
        P("tensor", None),
        P("tensor", None),
        P("dp", None, "tensor"),
        P("dp", None, "tensor"),
    )
    return jax.shard_map(
        on_device, mesh=mesh, in_specs=in_specs, out_specs=out_specs, check_vma=False
    )
```

```python
import functools

import jax
import jax.numpy as jnp
from jax import lax
from jax.experimental import pallas as pl
from jax.experimental.pallas import tpu as pltpu
from jax.sharding import PartitionSpec as P

MESH = pl.DeviceIdType.MESH
F32 = jnp.float32
BF16 = jnp.bfloat16
D = 4096
F = 128
RANK = 32
SUPERS = 8
ROWS = D // SUPERS
SUB = ROWS // 128
AHEAD = 5
CHIPS = 32
PLANE = 16
QUADS = 4


def far_first():
    offsets = [(dx, dy, dz) for dx in range(4) for dy in range(4) for dz in range(2) if dx + dy + dz > 0]
    offsets.sort(key=lambda o: -(min(o[0], 4 - o[0]) + min(o[1], 4 - o[1]) + o[2]))
    order = []
    for dx, dy, dz in offsets:
        for offset in ((dx, dy, dz), (-dx % 4, -dy % 4, dz)):
            if offset not in order:
                order.append(offset)
    return order


OFFSETS = far_first()


def nt(a, b):
    return lax.dot_general(a, b, (((1,), (1,)), ((), ())), preferred_element_type=F32)


def nn(a, b):
    return jnp.dot(a, b, preferred_element_type=F32)


def full(a, b):
    return jnp.dot(a, b, preferred_element_type=F32, precision=lax.Precision.HIGHEST)


def split(value):
    high = value.astype(BF16)
    return high, (value - high.astype(F32)).astype(BF16)


def thirds(value):
    high = value.astype(BF16)
    rest = value - high.astype(F32)
    mid = rest.astype(BF16)
    return high, mid, (rest - mid.astype(F32)).astype(BF16)


def tall_of(block):
    high, low = split(block)
    return jnp.concatenate([high.astype(F32), low.astype(F32)], axis=0).T.astype(BF16)


def wide_of(weight):
    high, low = split(weight)
    return jnp.concatenate([high, high, low, low], axis=0)


def low_rank(tall, wide):
    return nn(tall, wide[: 2 * RANK, :]) + nn(tall, wide[2 * RANK :, :])


def reduce_kernel(
    gk, gv, ek, ev, qk, qv,
    fed, left, result,
    stage, q_in, q_all, part, pair_in, ring_in, quad_in, share_in, shared, acc, gram_acc, t_plane, left_rows, own, spread,
    q_sem, load_sem, pair_send, pair_recv, ring_send, ring_recv, share_send, share_recv, quad_send, quad_recv,
    gather_send, gather_recv, pass_send, pass_recv, plane_send, plane_recv, last_send, last_recv,
):
    dp = lax.axis_index("dp")
    z = lax.axis_index("tensor")
    core = dp & 1
    chip = dp >> 1
    x = chip >> 2
    y = chip & 3
    shifted = (z + 8 - core) & 7
    bit = shifted & 1
    quad = shifted >> 1
    me = chip * 2 + bit
    xs = [(x + i) & 3 for i in range(4)]
    ys = [(y + i) & 3 for i in range(4)]
    bits = [bit, 1 - bit]
    partner = (chip * 2 + 1 - core, z)
    quads = [(dp, (z + 2 * i) & 7) for i in range(QUADS)]

    def device_at(offset):
        dx, dy, dz = offset
        return ((xs[dx] * 4 + ys[dy]) * 2 + core, (quad * 2 + bits[dz] + core) & 7)

    def block(step):
        inner = (step >= 2) & (step < 6)
        dx = jnp.where(step < 2, 2, jnp.where(inner, 1 + 2 * (step & 1), 0))
        half = jnp.where(inner, 2 - (step >> 1), 1 - (step & 1))
        return ((x + dx) & 3) * 2 + (((y >> 1) + half) & 1)

    def rows_of(b):
        return pl.ds(pl.multiple_of(b * ROWS, ROWS), ROWS)

    def slots_of(b):
        return pl.ds(b * SUB, SUB)

    def load(step, a, ref):
        rows = rows_of(block(step))
        return pltpu.make_async_copy(ref.at[0, rows], stage.at[a, rows], load_sem.at[step, a])

    def start_load(step, carry):
        for a, ref in enumerate((gk, gv, ek, ev)):
            load(step, a, ref).start()
        return carry

    q_loads = [pltpu.make_async_copy(q, q_in.at[m], q_sem.at[m]) for m, q in enumerate((qk, qv))]
    for q_load in q_loads:
        q_load.start()
    lax.fori_loop(0, 2, start_load, 0)

    barrier = pltpu.get_barrier_semaphore()
    for target in [device_at(offset) for offset in OFFSETS] + quads[1:] + [partner]:
        pl.semaphore_signal(barrier, inc=1, device_id=target, device_id_type=MESH)
    lax.fori_loop(2, SUPERS, start_load, 0)

    q_all[...] = jnp.zeros_like(q_all)
    for m in range(2):
        q_loads[m].wait()
        for part_of, piece in enumerate(split(q_in[m])):
            row = part_of * 2 * RANK + m * RANK
            q_all[row : row + RANK, m * F : (m + 1) * F] = piece

    def add_left(step, carry):
        b = block(step)
        rows = rows_of(b)
        for a, ref in enumerate((gk, gv, ek, ev)):
            load(step, a, ref).wait()
        highs, lows = [], []
        for m in range(2):
            value = stage[m, rows, :] + stage[2 + m, rows, :]
            fed[m, rows, :] = value
            high, low = split(value)
            highs.append(high)
            lows.append(low)
        high = jnp.concatenate(highs, axis=1)
        low = jnp.concatenate(lows, axis=1)
        product = nt(q_all[...], high)
        total = product[: 2 * RANK] + product[2 * RANK :] + nt(q_all[: 2 * RANK, :], low)
        for m in range(2):
            for j in range(SUB):
                part[m, b * SUB + j] = total[m * RANK : (m + 1) * RANK, j * 128 : (j + 1) * 128]
        return carry

    def pair_copy(step):
        at = slots_of(block(step))
        return pltpu.make_async_remote_copy(
            src_ref=part.at[1 - core, at], dst_ref=pair_in.at[at], send_sem=pair_send,
            recv_sem=pair_recv.at[step], device_id=partner, device_id_type=MESH)

    def ring_copy(member):
        target = ((member >> 1) * 2 + core, (quad * 2 + (member & 1) + core) & 7)
        return pltpu.make_async_remote_copy(
            src_ref=part.at[core, member], dst_ref=ring_in.at[me], send_sem=ring_send,
            recv_sem=ring_recv.at[chip >> 1], device_id=target, device_id_type=MESH)

    def scatter(step, kept):
        pair_copy(step).wait_recv()
        b = block(step)
        at = slots_of(b)
        part[core, at] = part[core, at] + pair_in[at]
        for dy in (1, 0):
            for dz in (1, 0):
                if (dy, dz) != (0, 0) or not kept:
                    ring_copy(b * SUB + ((y + dy) & 1) * 2 + bits[dz]).start()

    def start_pair(step, carry):
        pair_copy(step).start()
        return carry

    def overlapped(step, carry):
        add_left(step, 0)
        pair_copy(step).start()
        scatter(2 * (step - AHEAD), False)
        scatter(2 * (step - AHEAD) + 1, False)
        return carry

    lax.fori_loop(0, AHEAD, add_left, 0)
    pl.semaphore_wait(barrier, len(OFFSETS) + QUADS)
    for step in range(AHEAD):
        start_pair(step, 0)
    for step in range(AHEAD, SUPERS):
        overlapped(step, 0)
    for step in range(2 * (SUPERS - AHEAD), SUPERS - 1):
        scatter(step, False)
    scatter(SUPERS - 1, True)
    ring_in[me] = part[core, me]

    def share_copy(step):
        rows = rows_of(block(step))
        return pltpu.make_async_remote_copy(
            src_ref=fed.at[1 - core, rows], dst_ref=share_in.at[rows], send_sem=share_send,
            recv_sem=share_recv.at[step], device_id=partner, device_id_type=MESH)

    def start_share(step, carry):
        share_copy(step).start()
        return carry

    lax.fori_loop(0, SUPERS, start_share, 0)

    def share_step(step, carry):
        share_copy(step).wait_recv()
        rows = rows_of(block(step))
        high, low = split(fed[core, rows, :] + share_in[rows, :])
        shared[rows, :F] = high
        shared[rows, F:] = low
        return carry

    lax.fori_loop(0, SUPERS, share_step, 0)
    most = pl.ds(0, CHIPS - 1)
    total = jnp.zeros((RANK, 128), F32)
    for step in range(SUPERS):
        b = block(step)
        arrived = ring_in.at[pl.ds(b * SUB, SUB if step < SUPERS - 1 else SUB - 1)]
        pltpu.make_async_copy(arrived, arrived, ring_recv.at[b]).wait()
        total = total + jnp.sum(ring_in[slots_of(b)], axis=0)
    quad_in[quad] = total

    for i in (2, 1, 3):
        pltpu.make_async_remote_copy(
            src_ref=quad_in.at[quad], dst_ref=quad_in.at[quad], send_sem=quad_send, recv_sem=quad_recv,
            device_id=quads[i], device_id_type=MESH).start()
    three = pl.ds(0, QUADS - 1)
    pltpu.make_async_copy(quad_in.at[three], quad_in.at[three], quad_recv).wait()
    left[core, me] = (quad_in[0] + quad_in[1]) + (quad_in[2] + quad_in[3])

    for offset in OFFSETS:
        pltpu.make_async_remote_copy(
            src_ref=left.at[core, me], dst_ref=left.at[core, me], send_sem=gather_send,
            recv_sem=gather_recv.at[chip >> 1], device_id=device_at(offset), device_id_type=MESH).start()

    def pass_copy(step, side):
        at = slots_of(block(step))
        return pltpu.make_async_remote_copy(
            src_ref=left.at[side, at], dst_ref=left.at[side, at], send_sem=pass_send,
            recv_sem=pass_recv, device_id=partner, device_id_type=MESH)

    def left_block(m, b):
        high, low = split(jnp.concatenate([left[m, b * SUB + j] for j in range(SUB)], axis=1))
        return jnp.concatenate([high, low], axis=0)

    def gather(step, kept):
        b = block(step)
        arrived = left.at[core, pl.ds(b * SUB, SUB - 1 if kept else SUB)]
        pltpu.make_async_copy(arrived, arrived, gather_recv.at[b]).wait()
        acc[...] += nn(left_block(core, b), shared[rows_of(b), :])

    def digest(step):
        b = block(step)
        both = left_block(core, b)
        gram_acc[...] += nt(both, both)
        for j in range(SUB):
            rows = pl.ds(pl.multiple_of((b * SUB + j) * 128, 128), 128)
            left_rows[rows, : 2 * RANK] = tall_of(left[core, b * SUB + j])

    def gather_step(step, carry):
        gather(step, False)
        return carry

    acc[...] = jnp.zeros_like(acc)
    gram_acc[...] = jnp.zeros_like(gram_acc)
    for step in range(SUPERS - 1):
        gather(step, False)
    gather(SUPERS - 1, True)

    t_plane[chip] = acc[:RANK, :F] + (acc[RANK:, :F] + acc[:RANK, F:]) + acc[RANK:, F:]
    for dx, dy, dz in OFFSETS:
        if dz == 0:
            pltpu.make_async_remote_copy(
                src_ref=t_plane.at[chip], dst_ref=t_plane.at[chip], send_sem=plane_send, recv_sem=plane_recv,
                device_id=device_at((dx, dy, 0)), device_id_type=MESH).start()

    def start_pass(step, carry):
        pass_copy(step, core).start()
        return carry

    lax.fori_loop(0, SUPERS, start_pass, 0)

    def digest_step(step, carry):
        digest(step)
        return carry

    lax.fori_loop(0, SUPERS, digest_step, 0)
    products = gram_acc[...]
    gram = (products[:RANK, :RANK] + products[RANK:, RANK:]) + (products[:RANK, RANK:] + products[RANK:, :RANK])
    row = lax.broadcasted_iota(jnp.int32, (RANK, RANK), 0)
    column = lax.broadcasted_iota(jnp.int32, (RANK, RANK), 1)
    unit = jnp.where(row == column, 1.0, 0.0).astype(F32)
    work = jnp.concatenate([unit, gram, jnp.zeros((RANK, 2 * RANK), F32)], axis=1)
    wide_row = lax.broadcasted_iota(jnp.int32, (RANK, 4 * RANK), 0)
    wide_column = lax.broadcasted_iota(jnp.int32, (RANK, 4 * RANK), 1)
    pivots = jnp.ones((RANK, 1), F32)
    for j in range(RANK):
        picked = work[:, RANK + j : RANK + j + 1]
        pivot = picked[j : j + 1, :]
        pivots = jnp.where(wide_row[:, :1] == j, pivot, pivots)
        work = work - jnp.where(wide_row[:, :1] > j, picked / pivot, 0.0) * work[j : j + 1, :]
    inverse = (work * lax.rsqrt(pivots))[:, :RANK]
    square = jnp.concatenate([inverse, jnp.zeros((RANK, 3 * RANK), F32)], axis=1)
    upper = jnp.concatenate([square, jnp.zeros((3 * RANK, 4 * RANK), F32)], axis=0).T
    solver = jnp.concatenate([inverse, full(upper[:RANK, :RANK], inverse)], axis=0) * (1.0 / 32)
    s_high, s_mid, s_low = thirds(solver)
    spread[:, : 6 * RANK] = jnp.concatenate([s_high, s_high, s_mid, s_mid, s_high, s_low], axis=1)

    fifteen = pl.ds(0, PLANE - 1)
    pltpu.make_async_copy(t_plane.at[fifteen], t_plane.at[fifteen], plane_recv).wait()
    high, mid, low = thirds(jnp.sum(t_plane[...], axis=0))
    result[core] = nn(spread[:, : 6 * RANK], jnp.concatenate([high, mid, high, mid, low, high], axis=0))
    last = pltpu.make_async_remote_copy(
        src_ref=result.at[core], dst_ref=result.at[core], send_sem=last_send, recv_sem=last_recv,
        device_id=partner, device_id_type=MESH)
    last.start()

    own[...] = wide_of(result[core, RANK:])

    def own_step(b, carry):
        rows = rows_of(b)
        fed[core, rows, :] = fed[core, rows, :] - low_rank(left_rows[rows, : 2 * RANK], own)
        return carry

    lax.fori_loop(0, SUPERS, own_step, 0)

    for ref, sem in ((pair_in, pair_send), (share_in, share_send), (ring_in, pass_send), (ring_in, pass_recv)):
        pltpu.make_async_copy(ref, ref, sem).wait()
    pltpu.make_async_copy(ring_in.at[most], ring_in.at[most], ring_send).wait()
    pltpu.make_async_copy(quad_in.at[three], quad_in.at[three], quad_send).wait()
    pltpu.make_async_copy(ring_in.at[most], ring_in.at[most], gather_send).wait()
    pltpu.make_async_copy(t_plane.at[fifteen], t_plane.at[fifteen], plane_send).wait()
    last.wait()


def error_kernel(fed, left, result, right_key, right_value, new_key, new_value, wide, out, sem):
    core = lax.axis_index("dp") & 1
    news = (new_key, new_value)

    def write(m):
        done = pltpu.make_async_copy(fed.at[1 - m], news[1 - m].at[0], sem.at[SUPERS])
        done.start()
        right_key[...] = result[0, :RANK]
        right_value[...] = result[1, :RANK]
        wide[...] = wide_of(result[m, RANK:])
        copies = []
        for b in range(SUPERS):
            rows = slice(b * ROWS, (b + 1) * ROWS)
            tall = jnp.concatenate([tall_of(left[m, b * SUB + j]) for j in range(SUB)], axis=0)
            out[rows, :] = fed[m, rows, :] - low_rank(tall, wide)
            copies.append(pltpu.make_async_copy(out.at[rows], news[m].at[0, rows], sem.at[b]))
            copies[-1].start()
        for copy in copies:
            copy.wait()
        done.wait()

    for m in range(2):
        pl.when(core == 1 - m)(functools.partial(write, m))


def on_device(grad_key, grad_value, error_key, error_value, factor_key, factor_value):
    vmem = pl.BlockSpec(memory_space=pltpu.VMEM)
    anywhere = pl.BlockSpec(memory_space=pl.ANY)
    dma = pltpu.SemaphoreType.DMA
    fed, left, result = pl.pallas_call(
        reduce_kernel,
        out_shape=(
            pltpu.VMEM((2, D, F), F32),
            pltpu.VMEM((2, CHIPS, RANK, 128), F32),
            pltpu.VMEM((2, 2 * RANK, F), F32),
        ),
        in_specs=[anywhere] * 6,
        out_specs=(vmem,) * 3,
        scratch_shapes=[
            pltpu.VMEM((4, D, F), F32),
            pltpu.VMEM((2, RANK, F), F32),
            pltpu.VMEM((4 * RANK, 2 * F), BF16),
            pltpu.VMEM((2, CHIPS, RANK, 128), F32),
            pltpu.VMEM((CHIPS, RANK, 128), F32),
            pltpu.VMEM((CHIPS, RANK, 128), F32),
            pltpu.VMEM((QUADS, RANK, 128), F32),
            pltpu.VMEM((D, F), F32),
            pltpu.VMEM((D, 2 * F), BF16),
            pltpu.VMEM((2 * RANK, 2 * F), F32),
            pltpu.VMEM((2 * RANK, 2 * RANK), F32),
            pltpu.VMEM((PLANE, RANK, F), F32),
            pltpu.VMEM((D, 4 * RANK), BF16),
            pltpu.VMEM((4 * RANK, F), BF16),
            pltpu.VMEM((2 * RANK, 8 * RANK), BF16),
            dma((2,)),
            dma((SUPERS, 4)),
            dma,
            dma((SUPERS,)),
            dma,
            dma((SUPERS,)),
            dma,
            dma((SUPERS,)),
            dma,
            dma,
            dma,
            dma((SUPERS,)),
            dma,
            dma,
            dma,
            dma,
            dma,
            dma,
        ],
        compiler_params=pltpu.CompilerParams(
            collective_id=0, has_side_effects=True, vmem_limit_bytes=32 * 2**20
        ),
        cost_estimate=pl.CostEstimate(flops=10**9, bytes_accessed=12 * 2**20, transcendentals=0),
        name="reduce_factors",
    )(*(pltpu.with_memory_space_constraint(a, pltpu.HBM) for a in (grad_key, grad_value, error_key, error_value, factor_key.T, factor_value.T)))
    right_key, right_value, new_key, new_value = pl.pallas_call(
        error_kernel,
        out_shape=(
            jax.ShapeDtypeStruct((RANK, F), F32),
            jax.ShapeDtypeStruct((RANK, F), F32),
            jax.ShapeDtypeStruct((1, D, F), F32),
            jax.ShapeDtypeStruct((1, D, F), F32),
        ),
        in_specs=[vmem] * 3,
        out_specs=(vmem, vmem, anywhere, anywhere),
        scratch_shapes=[
            pltpu.VMEM((4 * RANK, F), BF16),
            pltpu.VMEM((D, F), F32),
            dma((SUPERS + 1,)),
        ],
        compiler_params=pltpu.CompilerParams(vmem_limit_bytes=32 * 2**20),
        cost_estimate=pl.CostEstimate(flops=10**9, bytes_accessed=8 * 2**20, transcendentals=0),
        name="new_errors",
    )(fed, left, result)
    return right_key.T, right_value.T, new_key, new_value


def solution(mesh):
    in_specs = (
        P("dp", None, "tensor"),
        P("dp", None, "tensor"),
        P("dp", None, "tensor"),
        P("dp", None, "tensor"),
        P("tensor", None),
        P("tensor", None),
    )
    out_specs = (
        P("tensor", None),
        P("tensor", None),
        P("dp", None, "tensor"),
        P("dp", None, "tensor"),
    )
    return jax.shard_map(
        on_device, mesh=mesh, in_specs=in_specs, out_specs=out_specs, check_vma=False
    )
```
